128 devices in a mesh: chan: 4 (over x), blk: 32 (over z, y, core).
Axes of the slice: x: 4, y: 4, z: 4, core: 2. Of those that a mesh axis runs over, the one named last changes fastest.
Arguments:
- coeffs: bfloat16 [12, 2, 3072, 1536], P('chan', None, 'blk'), may hold values from -0.15 to 0.15
- legendre: bfloat16 [4, 768, 256, 1536], P('chan', 'blk'), may hold values from -0.15625 to 0.15625
- m_order: int32 [3072], replicated, may hold values from 0 to 3071, as said below
- sector_len: int32 [512, 16], P(('chan', 'blk')), may hold values from 256 to 4352, as said below
Outputs:
- ilc_map: float32 [512, 8192], P(('chan', 'blk'))
The draws below stay inside these ranges and needn't reach their ends.
Inputs may be any that keep to these rules, and one draw needn't show every extreme that they name: `m_order`: a permutation of 0 to 3071; slots 2 j and 2 j + 1 hold the orders m and 3071 - m. `sector_len`: the 16 lengths of each cycle sum to 8192.
All inputs are finite; a program needn't handle non-finite values.
Results may differ from the reference program's by a relative error of at most 0.0003.
Values may be sent and summed in bfloat16 or wider, within the bound.
No kernel may reach another device: no remote copies, remote signals or barrier semaphores. Data moves between devices by JAX's collectives and lax.ppermute only.
A program may use at most 256 MiB of HBM per device.

```python
import jax
import jax.numpy as jnp
from jax import lax

CH = 12
M = 3072
LB = 1536
PIX = 8192
NSEC = 16
RN = 256
GROUPS = 4
N_CHAN = 4
N_BLK = 32


def draw_coeffs(key, part):
    shape_all = (CH, 2, M, LB)
    common_key = jax.random.fold_in(key, 101)
    noise_key = jax.random.fold_in(key, 202)
    spread_key = jax.random.fold_in(key, 303)
    common = jax.random.truncated_normal(common_key, -4.0, 4.0, (1, 2, M, LB), jnp.float32)
    noise_part = jax.random.truncated_normal(noise_key, -4.0, 4.0, shape_all, jnp.float32)
    spread = jnp.exp(jax.random.uniform(spread_key, (CH, 1, 1, 1), jnp.float32, -0.6931472, 0.6931472))
    return (0.0125 * (common + spread * noise_part)).astype(jnp.bfloat16)


def draw_m_order(key, part):
    pair_low = jax.random.permutation(key, M // 2).astype(jnp.int32)
    return jnp.stack([pair_low, M - 1 - pair_low], axis=1).reshape(M).astype(jnp.int32)


def draw_sector_len(key, part):
    cycle_count = 2 * RN
    spare_pixels = PIX // 2
    least_length = PIX // (2 * NSEC)
    inner_cuts = jax.random.randint(jax.random.fold_in(key, 7), (cycle_count, NSEC - 2), 0, spare_pixels + 1, dtype=jnp.int32)
    keep_rows = (jnp.arange(cycle_count, dtype=jnp.int32) > 0).astype(jnp.int32)
    inner_cuts = inner_cuts * keep_rows[:, None]
    cut_points = jnp.sort(jnp.concatenate([jnp.zeros((cycle_count, 1), jnp.int32), inner_cuts], axis=1), axis=1)
    bounds = jnp.concatenate([cut_points, jnp.full((cycle_count, 1), spare_pixels, jnp.int32)], axis=1)
    extra_pixels = bounds - jnp.concatenate([jnp.zeros((cycle_count, 1), jnp.int32), bounds[:, :-1]], axis=1)
    lengths = least_length + extra_pixels
    offset = jax.random.randint(jax.random.fold_in(key, 9), (cycle_count, 1), 0, NSEC, dtype=jnp.int32)
    rotation = (jnp.arange(NSEC, dtype=jnp.int32)[None, :] + offset) % NSEC
    return jnp.take_along_axis(lengths, rotation, axis=1).astype(jnp.int32)


def block_levels(rng, shape, split, smallest, high):
    gain, own = 1.0, jax.random.fold_in(rng, 6)
    for axis_at, shards_of in split:
        draws = jnp.exp(jax.random.uniform(jax.random.fold_in(own, axis_at), (shards_of,), jnp.float32, smallest / len(split), high / len(split)))
        gain = gain * jnp.repeat(draws, shape[axis_at] // shards_of).reshape([-1 if axis == axis_at else 1 for axis in range(len(shape))])
    return gain


def normal_values(key, extent, deviation, limit, split=(), kind=jnp.bfloat16):
    values = deviation * jax.random.normal(key, extent, jnp.float32)
    if split:
        values = values * block_levels(key, extent, split, -0.22, 0.18)
    return jnp.clip(values, -limit, limit).astype(kind)


def setup_inputs(seed: int = 0) -> dict:
    streams_of = jax.random.split(jax.random.key(seed), 5)
    coeffs = draw_coeffs(jax.random.fold_in(streams_of[4], 71), 0)
    legendre = normal_values(streams_of[1], (GROUPS, M // GROUPS, RN, LB), LB ** -0.5, 0.15625, ((0, 4), (1, 32)))
    m_order = draw_m_order(jax.random.fold_in(streams_of[4], 71), 0)
    sector_len = draw_sector_len(jax.random.fold_in(streams_of[4], 71), 0)
    return {"coeffs": coeffs, "legendre": legendre, "m_order": m_order, "sector_len": sector_len}


RIDGE_FACTOR = 0.05
TWO_PI = 6.283185307179586

def legendre_block(coeff_block, operator, orders):
    highest = lax.Precision.HIGHEST
    degree = M - LB + lax.iota(jnp.int32, LB)
    valid_mask = degree[None, :] >= orders[:, None]
    odd_mask = (degree[None, :] + orders[:, None]) % 2 == 1
    zero_value = jnp.zeros((), coeff_block.dtype)
    even_part = jnp.where((valid_mask & ~odd_mask)[None, None], coeff_block, zero_value)
    odd_part = jnp.where((valid_mask & odd_mask)[None, None], coeff_block, zero_value)
    operator_wide = operator.astype(jnp.float32)
    even_sum = jnp.einsum('cpsl,srl->cprs', even_part.astype(jnp.float32), operator_wide, precision=highest)
    odd_sum = jnp.einsum('cpsl,srl->cprs', odd_part.astype(jnp.float32), operator_wide, precision=highest)
    return jnp.concatenate([even_sum + odd_sum, even_sum - odd_sum], axis=2)

def cycle_synthesis(spectra, orders):
    highest = lax.Precision.HIGHEST
    order_count = spectra.shape[-1]
    fine_count = 128
    coarse_count = PIX // fine_count
    coarse_phase = (lax.iota(jnp.int32, coarse_count) * fine_count)[:, None] * orders[None, :] % PIX
    fine_phase = orders[:, None] * lax.iota(jnp.int32, fine_count)[None, :] % PIX
    coarse_angle = coarse_phase.astype(jnp.float32) * (TWO_PI / PIX)
    fine_angle = fine_phase.astype(jnp.float32) * (TWO_PI / PIX)
    weight = jnp.where(orders == 0, 1.0, 2.0).astype(jnp.float32)
    coarse_cos = jnp.cos(coarse_angle)
    coarse_sin = jnp.sin(coarse_angle)
    fine_cos = weight[:, None] * jnp.cos(fine_angle)
    fine_sin = weight[:, None] * jnp.sin(fine_angle)
    real_part = spectra[:, 0].reshape(-1, 1, order_count)
    imag_part = spectra[:, 1].reshape(-1, 1, order_count)
    shifted_real = (real_part * coarse_cos[None] - imag_part * coarse_sin[None]).reshape(-1, order_count)
    shifted_imag = (real_part * coarse_sin[None] + imag_part * coarse_cos[None]).reshape(-1, order_count)
    result = jnp.dot(shifted_real.astype(jnp.float32), fine_cos.astype(jnp.float32), precision=highest, preferred_element_type=jnp.float32)
    result = result - jnp.dot(shifted_imag.astype(jnp.float32), fine_sin.astype(jnp.float32), precision=highest, preferred_element_type=jnp.float32)
    return result.reshape(spectra.shape[0], spectra.shape[2], PIX)

def cycle_combine(cycle_map, lengths):
    highest = lax.Precision.HIGHEST
    channel_count = cycle_map.shape[0]
    sector_end = jnp.cumsum(lengths).astype(jnp.int32)
    sector_start = (sector_end - lengths).astype(jnp.int32)
    pixels = lax.iota(jnp.int32, PIX)
    member = ((pixels[None, :] >= sector_start[:, None]) & (pixels[None, :] < sector_end[:, None])).astype(jnp.float32)
    products = (cycle_map[:, None, :] * cycle_map[None, :, :]).reshape(channel_count * channel_count, PIX)
    moments = jnp.einsum('qx,kx->kq', products, member, precision=highest)
    covariance = moments.reshape(-1, channel_count, channel_count) / lengths.astype(jnp.float32)[:, None, None]
    trace_part = jnp.trace(covariance, axis1=1, axis2=2) * (RIDGE_FACTOR / channel_count)
    regular = covariance + trace_part[:, None, None] * jnp.eye(channel_count, dtype=jnp.float32)
    factor = jnp.linalg.cholesky(regular)
    unit_rhs = jnp.ones((covariance.shape[0], channel_count, 1), jnp.float32)
    forward = lax.linalg.triangular_solve(factor, unit_rhs, left_side=True, lower=True)
    solved = lax.linalg.triangular_solve(factor, forward, left_side=True, lower=True, transpose_a=True)[:, :, 0]
    weights = solved / jnp.sum(solved, axis=1, keepdims=True)
    pixel_weights = jnp.einsum('ka,kx->ax', weights, member, precision=highest)
    return jnp.sum(pixel_weights * cycle_map, axis=0)

def reference(coeffs, legendre, m_order, sector_len):
    slot_count = M // (N_CHAN * N_BLK)
    block_span = N_CHAN * slot_count

    def one_block(block_number):
        coeff_block = lax.dynamic_slice_in_dim(coeffs, block_number * block_span, block_span, 2)
        operator = lax.dynamic_slice_in_dim(legendre, block_number * slot_count, slot_count, 1)
        operator = operator.reshape(block_span, RN, LB)
        orders = lax.dynamic_slice_in_dim(m_order, block_number * block_span, block_span, 0)
        return legendre_block(coeff_block, operator, orders)
    blocks = lax.map(one_block, jnp.arange(N_BLK, dtype=jnp.int32))
    spectra = jnp.moveaxis(blocks, 0, 3).reshape(CH, 2, 2 * RN, M)
    cycle_maps = lax.map(lambda channel: cycle_synthesis(channel[None], m_order)[0], spectra)
    return lax.map(lambda cycle_pair: cycle_combine(cycle_pair[0], cycle_pair[1]), (jnp.moveaxis(cycle_maps, 1, 0), sector_len))
```

```python
import functools

import jax
import jax.numpy as jnp
import ml_dtypes
import numpy as np
from jax import lax
from jax.experimental import pallas as pl
from jax.experimental.pallas import tpu as pltpu
from jax.sharding import PartitionSpec as P

M = 3072
LB = 1536
PIX = 8192
CH = 12
NSEC = 16
NSLOT = 24
NCYC = 4
N_CHAN = 4
N_BLK = 32
N_DEV = N_CHAN * N_BLK
RIDGE_FACTOR = 0.05

NA, NB, NM1, NM2 = 128, 64, 128, 24
ROWS = 18

f32, bf16 = jnp.float32, jnp.bfloat16


def split_np(x):
    high = x.astype(ml_dtypes.bfloat16)
    low = (x - high.astype(np.float64)).astype(ml_dtypes.bfloat16)
    return high, low


@functools.cache
def tables():
    b, m2 = np.arange(NB)[:, None], np.arange(NM2)[None, :]
    angle = 2 * np.pi * ((b * m2) % 64) / 64
    stage1 = np.block([[np.cos(angle), -np.sin(angle)], [np.sin(angle), np.cos(angle)]])
    high, low = split_np(stage1)
    stage1 = np.concatenate([high, high, low], axis=1)
    m1 = np.arange(NM1)[None, :]
    angle = 2 * np.pi * b * m1 / PIX
    twiddle = np.concatenate([np.cos(angle), np.sin(angle)], axis=0).astype(np.float32)
    m1, a = np.arange(NM1)[:, None], np.arange(NA)[None, :]
    angle = 2 * np.pi * ((m1 * a) % 128) / 128
    stage2 = 2.0 * np.concatenate([np.cos(angle), -np.sin(angle)], axis=0)
    stage2 = np.concatenate(split_np(stage2), axis=1)
    return stage1, twiddle, stage2


def split2(x):
    high = x.astype(bf16)
    return high, (x - high.astype(f32)).astype(bf16)


def split3(x):
    high = x.astype(bf16)
    rest = x - high.astype(f32)
    mid = rest.astype(bf16)
    return high, mid, (rest - mid.astype(f32)).astype(bf16)


def dot_nn(x, y):
    return lax.dot_general(x, y, (((1,), (0,)), ((), ())), preferred_element_type=f32)


def dot_nt(x, y):
    return lax.dot_general(x, y, (((1,), (1,)), ((), ())), preferred_element_type=f32)


def legendre_kernel(orders_ref, coef_ref, leg_ref, out_ref, wide_ref, acc_ref):
    step = pl.program_id(0)

    @pl.when(step == 0)
    def _():
        def widen(i, carry):
            value = coef_ref[i].astype(f32)
            for j in range(LB // 128):
                wide_ref[j, pl.ds(i * NSLOT, NSLOT), :] = value[:, j * 128 : (j + 1) * 128]
            return carry

        lax.fori_loop(0, 2 * CH, widen, 0)

    degree = (M - LB) + lax.broadcasted_iota(jnp.int32, (1, LB), 1)
    lane = lax.broadcasted_iota(jnp.int32, (64, 128), 1)
    half = lane < 64
    even_group = (lane & 32) == 0
    spare = (lane & 31) >= 24
    north, south = [], []
    for u in range(4):
        slot = step * 4 + u
        m = orders_ref[slot]
        coef = jnp.concatenate([wide_ref[j, pl.ds(slot, 2 * CH, stride=NSLOT), :] for j in range(LB // 128)], axis=1)
        keep = (degree >= m).astype(f32)
        sign = (1 - 2 * ((degree + m) & 1)).astype(f32) * keep
        none = jnp.zeros((8, LB), f32)
        up = jnp.concatenate([coef * keep, none], axis=0).astype(bf16)
        down = jnp.concatenate([coef * sign, none], axis=0).astype(bf16)
        rhs = jnp.concatenate([up, up, down, down], axis=0)
        acc_ref[u] = dot_nt(leg_ref[u], rhs)
        k0, k1, k2, k3 = (acc_ref[u, pl.ds(k, 64, stride=4), :] for k in range(4))
        first = jnp.where(even_group, k0, k1)
        second = jnp.where(even_group, k2, k3)
        north.append(jnp.where(half, first, pltpu.roll(second, 64, 1)))
        south.append(jnp.where(half, pltpu.roll(first, 64, 1), second))
    for hemi, part in enumerate((north, south)):
        for r in range(3):
            row = jnp.where(spare, pltpu.roll(part[3], 24 - 8 * r, 1), part[r])
            out_ref[pl.ds(hemi * 64 * ROWS + 3 * step + r, 64, stride=ROWS), :] = row


def legendre_call(orders, coef, legendre):
    return pl.pallas_call(
        legendre_kernel,
        out_shape=jax.ShapeDtypeStruct((N_DEV * ROWS, 128), f32),
        grid=(NSLOT // 4,),
        in_specs=[
            pl.BlockSpec(memory_space=pltpu.SMEM),
            pl.BlockSpec((2 * CH, NSLOT, LB), lambda i: (0, 0, 0)),
            pl.BlockSpec((4, 256, LB), lambda i: (i, 0, 0)),
        ],
        out_specs=pl.BlockSpec((N_DEV * ROWS, 128), lambda i: (0, 0)),
        scratch_shapes=[
            pltpu.VMEM((LB // 128, 2 * CH * NSLOT, 128), f32),
            pltpu.VMEM((4, 256, 128), f32),
        ],
        compiler_params=pltpu.CompilerParams(vmem_limit_bytes=40 * 2**20),
    )(orders, coef, legendre)


def map_kernel(
    orders_ref, lens_ref, data_ref, lane_len_ref, stage1_ref, twiddle_ref, stage2_ref, out_ref,
    last_ref, place_ref, turned_ref, map_ref, low_ref, high_ref, hot_ref, cov_ref, comb_ref, final_ref,
):
    lane = lax.broadcasted_iota(jnp.int32, (8, 128), 1)
    group = (lane & 31) >> 3

    def gather_last(i, carry):
        rows = [data_ref[pl.ds(i * 192 + r, 64, stride=3), :] for r in range(3)]
        wide = lax.broadcasted_iota(jnp.int32, (64, 128), 1)
        which = (wide & 31) >> 3
        rolled = [pltpu.roll(rows[r], 128 - (24 - 8 * r), 1) for r in range(3)]
        value = jnp.where(which == 0, rolled[0], jnp.where(which == 1, rolled[1], rolled[2]))
        last_ref[pl.ds(pl.multiple_of(i * 64, 64), 64), :] = value
        return carry

    lax.fori_loop(0, 12, gather_last, 0)

    def place(src, carry):
        base = ((src & (N_BLK - 1)) * N_CHAN + (src >> 5)) * NSLOT
        for t in range(6):
            for r in range(3):
                m = orders_ref[base + 4 * t + r]
                place_ref[pl.ds(m, 1), :] = data_ref[pl.ds(src * ROWS + 3 * t + r, 1), :]
            m = orders_ref[base + 4 * t + 3]
            place_ref[pl.ds(m, 1), :] = last_ref[pl.ds(src * 6 + t, 1), :]
        return carry

    lax.fori_loop(0, N_DEV, place, 0)
    place_ref[0:1, :] = place_ref[0:1, :] * 0.5

    for m2 in range(NM2):
        block = place_ref[m2 * 128 : (m2 + 1) * 128, :].T
        for k in range(NCYC):
            turned_ref[pl.ds(k * 2 * CH * NM2 + m2, 2 * CH, stride=NM2), :] = block[k * 32 : k * 32 + 24]

    stage1 = stage1_ref[...]

    def transform(i, carry):
        parts = []
        for j in range(2):
            high, low = split2(turned_ref[pl.ds(pl.multiple_of(i * 96 + j * 48, 16), 48), :])
            parts.append(jnp.concatenate([high, low, high], axis=0))
        inner = dot_nn(stage1, jnp.concatenate(parts, axis=1))
        tc, ts = twiddle_ref[0:64, :], twiddle_ref[64:128, :]
        outer = []
        for j in range(2):
            re, im = inner[0:64, j * 128 : (j + 1) * 128], inner[64:128, j * 128 : (j + 1) * 128]
            outer.append(jnp.concatenate([re * tc - im * ts, re * ts + im * tc], axis=1))
        high, low = split2(jnp.concatenate(outer, axis=0))
        both = dot_nn(high, stage2_ref[...])
        maps = both[:, 0:128] + (both[:, 128:256] + dot_nn(low, stage2_ref[:, 0:128]))
        map_ref[pl.ds(pl.multiple_of(i * 128, 128), 128), :] = maps
        return carry

    lax.fori_loop(0, NCYC * CH // 2, transform, 0)

    chunk = lax.broadcasted_iota(jnp.int32, (64, 128), 1)
    offset = lax.broadcasted_iota(jnp.int32, (64, 128), 0)
    low_ref[...] = jnp.zeros_like(low_ref)
    high_ref[...] = jnp.zeros_like(high_ref)
    cov_ref[...] = jnp.zeros_like(cov_ref)

    def sectors(k):
        start = chunk * 64
        which = jnp.zeros((64, 128), jnp.int32)
        bound = jnp.full((64, 128), PIX, jnp.int32)
        end = jnp.int32(0)
        for q in range(NSEC):
            end = end + lens_ref[k, q]
            passed = end <= start
            which = which + passed.astype(jnp.int32)
            bound = jnp.minimum(bound, jnp.where(passed, PIX, end))
        return which, start + offset < bound

    def moments(k, carry):
        which, inside = sectors(k)
        row = lax.broadcasted_iota(jnp.int32, (64, 128), 0)
        own = (row >> 4) == k
        hot_low = (own & ((row & 15) == which)).astype(bf16)
        hot_high = (own & ((row & 15) == which + 1)).astype(bf16)
        hot_ref[pl.ds(pl.multiple_of(k * 128, 128), 64), :] = hot_low
        hot_ref[pl.ds(pl.multiple_of(k * 128 + 64, 64), 64), :] = hot_high
        base = pl.multiple_of(k * CH * 64, 64)
        for i in range(CH):
            value = map_ref[pl.ds(base + i * 64, 64), :]
            low = jnp.where(inside, value, 0.0)
            high = jnp.where(inside, 0.0, value)
            for j in range(i, CH):
                other = map_ref[pl.ds(base + j * 64, 64), :]
                for part, ref in ((low, low_ref), (high, high_ref)):
                    total = jnp.sum(part * other, axis=0, keepdims=True)
                    ref[i * 16 + j : i * 16 + j + 1, :] = total
                    if i != j:
                        ref[j * 16 + i : j * 16 + i + 1, :] = total
        total = cov_ref[...]
        for ref, hot in ((low_ref, hot_low), (high_ref, hot_high)):
            for part in split3(ref[...]):
                total = total + dot_nt(part, hot)
        cov_ref[...] = total
        return carry

    lax.fori_loop(0, NCYC, moments, 0)

    scale = 1.0 / lane_len_ref[...].astype(f32)
    sub = lax.broadcasted_iota(jnp.int32, (16, 64), 0)
    mat = [cov_ref[i * 16 : (i + 1) * 16, :] * scale for i in range(CH)]
    trace = mat[0][0:1]
    for i in range(1, CH):
        trace = trace + mat[i][i : i + 1]
    ridge = trace * (RIDGE_FACTOR / CH)
    for i in range(CH):
        mat[i] = jnp.where(sub == CH, 1.0, jnp.where(sub == i, mat[i] + ridge, mat[i]))
    for p in range(CH):
        pivot = mat[p] / mat[p][p : p + 1]
        for i in range(CH):
            mat[i] = pivot if i == p else mat[i] - mat[i][p : p + 1] * pivot
    solved = [mat[i][CH : CH + 1] for i in range(CH)]
    norm = solved[0]
    for i in range(1, CH):
        norm = norm + solved[i]
    weights = jnp.concatenate([s / norm for s in solved] + [jnp.zeros((4, 64), f32)], axis=0)
    weight_parts = split3(weights)

    def combine(k, carry):
        _, inside = sectors(k)
        chunk_weights = []
        for h in range(2):
            hot = hot_ref[pl.ds(pl.multiple_of(k * 128 + h * 64, 64), 64), :]
            chunk_weights.append(sum(dot_nn(part, hot) for part in weight_parts))
        base = pl.multiple_of(k * CH * 64, 64)
        total = jnp.zeros((64, 128), f32)
        for c in range(CH):
            weight = jnp.where(inside, chunk_weights[0][c : c + 1], chunk_weights[1][c : c + 1])
            total = total + weight * map_ref[pl.ds(base + c * 64, 64), :]
        wide = jnp.concatenate([total, total], axis=0).T
        comb_ref[...] = wide
        pair = jnp.where(chunk < 64, comb_ref[pl.ds(0, 64, stride=2), :], comb_ref[pl.ds(1, 64, stride=2), :])
        out_ref[k] = pair
        return carry

    lax.fori_loop(0, NCYC, combine, 0)


def map_call(orders, lens, data):
    stage1, twiddle, stage2 = tables()
    smem, vmem = pl.BlockSpec(memory_space=pltpu.SMEM), pl.BlockSpec(memory_space=pltpu.VMEM)
    return pl.pallas_call(
        map_kernel,
        out_shape=jax.ShapeDtypeStruct((NCYC, 64, 128), f32),
        in_specs=[smem, smem] + [vmem] * 5,
        out_specs=vmem,
        scratch_shapes=[
            pltpu.VMEM((N_DEV * 6, 128), f32),
            pltpu.VMEM((M, 128), f32),
            pltpu.VMEM((NCYC * 2 * CH * NM2, 128), f32),
            pltpu.VMEM((NCYC * CH * 64, 128), f32),
            pltpu.VMEM((CH * 16, 128), f32),
            pltpu.VMEM((CH * 16, 128), f32),
            pltpu.VMEM((NCYC * 128, 128), bf16),
            pltpu.VMEM((CH * 16, 64), f32),
            pltpu.VMEM((128, 128), f32),
            pltpu.VMEM((8, 128), f32),
        ],
        compiler_params=pltpu.CompilerParams(vmem_limit_bytes=40 * 2**20),
    )(orders, lens, data, lens.reshape(1, NCYC * NSEC), stage1, twiddle, stage2)


def per_device(coeffs, legendre, m_order, sector_len):
    first_slot = (lax.axis_index("blk") * N_CHAN + lax.axis_index("chan")) * NSLOT
    orders = lax.dynamic_slice_in_dim(m_order, first_slot, NSLOT, 0)
    parts = jnp.moveaxis(coeffs.reshape(3, 2, N_CHAN, NSLOT, LB), 2, 0)
    parts = lax.all_to_all(parts, "chan", 0, 0, tiled=True)
    sent = legendre_call(orders, parts.reshape(2 * CH, NSLOT, LB), legendre[0])
    data = lax.all_to_all(sent.reshape(N_DEV, 1, ROWS * 128), ("chan", "blk"), 0, 0, tiled=True)
    out = map_call(m_order, sector_len, data.reshape(N_DEV * ROWS, 128))
    return out.reshape(NCYC, PIX)


def solution(mesh):
    placed = (
        P("chan", None, "blk", None),
        P("chan", "blk", None, None),
        P(),
        P(("chan", "blk"), None),
    )
    return jax.shard_map(
        per_device, mesh=mesh, in_specs=placed, out_specs=P(("chan", "blk"), None), check_vma=False
    )
```

```python
import functools

import jax
import jax.numpy as jnp
import ml_dtypes
import numpy as np
from jax import lax
from jax.experimental import pallas as pl
from jax.experimental.pallas import tpu as pltpu
from jax.sharding import PartitionSpec as P

M = 3072
LB = 1536
PIX = 8192
CH = 12
NSEC = 16
NSLOT = 24
NCYC = 4
N_CHAN = 4
N_BLK = 32
N_DEV = N_CHAN * N_BLK
RIDGE_FACTOR = 0.05

NA, NB, NM1, NM2 = 128, 64, 128, 24
PAIRS = 6
ROWS = 10

CHUNKS = (16, 8)
VMEM_LEG = 16 * 2**20
FETCHES = 6
TOP_CODE = 32000.0
LN2 = float(np.log(2.0))

f32, bf16 = jnp.float32, jnp.bfloat16


def split_np(x):
    high = x.astype(ml_dtypes.bfloat16)
    low = (x - high.astype(np.float64)).astype(ml_dtypes.bfloat16)
    return high, low


@functools.cache
def tables():
    b, m2 = np.arange(NB)[:, None], np.arange(NM2)[None, :]
    angle = 2 * np.pi * ((b * m2) % 64) / 64
    stage1 = np.block([[np.cos(angle), -np.sin(angle)], [np.sin(angle), np.cos(angle)]])
    high, low = split_np(stage1)
    stage1 = np.concatenate([high, high, low], axis=1)
    m1 = np.arange(NM1)[None, :]
    angle = 2 * np.pi * b * m1 / PIX
    twiddle = np.concatenate([np.cos(angle), np.sin(angle)], axis=0).astype(np.float32)
    m1, a = np.arange(NM1)[:, None], np.arange(NA)[None, :]
    angle = 2 * np.pi * ((m1 * a) % 128) / 128
    stage2 = 2.0 * np.concatenate([np.cos(angle), -np.sin(angle)], axis=0)
    stage2 = np.concatenate(split_np(stage2), axis=1)
    return stage1, twiddle, stage2


def split2(x):
    high = x.astype(bf16)
    return high, (x - high.astype(f32)).astype(bf16)


def split3(x):
    high = x.astype(bf16)
    rest = x - high.astype(f32)
    mid = rest.astype(bf16)
    return high, mid, (rest - mid.astype(f32)).astype(bf16)


def dot_nn(x, y):
    return lax.dot_general(x, y, (((1,), (0,)), ((), ())), preferred_element_type=f32)


def dot_nt(x, y):
    return lax.dot_general(x, y, (((1,), (1,)), ((), ())), preferred_element_type=f32)


def fetch_kernel(source_ref, out_ref, sems):
    step = NSLOT // FETCHES
    copies = [
        pltpu.make_async_copy(source_ref.at[pl.ds(i * step, step)], out_ref.at[pl.ds(i * step, step)], sems.at[i])
        for i in range(FETCHES)
    ]
    for copy in copies:
        copy.start()
    for copy in copies:
        copy.wait()


def fetch_call(legendre):
    return pl.pallas_call(
        fetch_kernel,
        out_shape=jax.ShapeDtypeStruct(legendre.shape, legendre.dtype),
        in_specs=[pl.BlockSpec(memory_space=pl.ANY)],
        out_specs=pl.BlockSpec(memory_space=pltpu.VMEM),
        scratch_shapes=[pltpu.SemaphoreType.DMA((FETCHES,))],
        compiler_params=pltpu.CompilerParams(vmem_limit_bytes=VMEM_LEG),
        cost_estimate=pl.CostEstimate(flops=0, bytes_accessed=2 * legendre.size * 2, transcendentals=0),
    )(legendre)


def legendre_kernel(first, count, has_before, orders_ref, *refs):
    coef_refs, refs = refs[:4], refs[4:]
    leg_ref, refs = refs[0], refs[1:]
    before_ref, refs = (refs[0], refs[1:]) if has_before else (None, refs)
    out_ref, wide_ref, acc_ref = refs

    me = lax.axis_index("chan")
    own = (lax.axis_index("blk") * N_CHAN + me) * NSLOT + first

    for k in range(4):
        source = (me - k) & (N_CHAN - 1)
        for i in range(6):
            value = coef_refs[k][i].astype(f32)
            start = pl.multiple_of((source * 6 + i) * count, 8)
            for j in range(LB // 128):
                wide_ref[j, pl.ds(start, count), :] = value[:, j * 128 : (j + 1) * 128]
    if has_before:
        out_ref[...] = before_ref[...]
    else:
        out_ref[...] = jnp.zeros_like(out_ref)

    degree = (M - LB) + lax.broadcasted_iota(jnp.int32, (1, LB), 1)
    lane = lax.broadcasted_iota(jnp.int32, (64, 128), 1)
    half = lane < 64
    even_group = (lane & 32) == 0
    spare = (lane & 31) >= 24

    def octet(step, carry):
        north, south = [], []
        for u in range(8):
            slot = step * 8 + u
            m = orders_ref[own + slot]
            coef = jnp.concatenate(
                [wide_ref[j, pl.ds(slot, 2 * CH, stride=count), :] for j in range(LB // 128)], axis=1
            )
            keep = (degree >= m).astype(f32)
            sign = (1 - 2 * ((degree + m) & 1)).astype(f32) * keep
            none = jnp.zeros((8, LB), f32)
            up = jnp.concatenate([coef * keep, none], axis=0).astype(bf16)
            down = jnp.concatenate([coef * sign, none], axis=0).astype(bf16)
            rhs = jnp.concatenate([up, up, down, down], axis=0)
            acc_ref[u] = dot_nt(leg_ref[first + slot], rhs)
        top = jnp.maximum(jnp.abs(acc_ref[0]), jnp.abs(acc_ref[1]))
        for u in range(2, 8):
            top = jnp.maximum(top, jnp.abs(acc_ref[u]))
        top = jnp.max(jnp.max(top, axis=0, keepdims=True), axis=1, keepdims=True)
        top = jnp.broadcast_to(jnp.maximum(top, 1e-30), (8, 128))
        code = jnp.ceil(jnp.log(top) * (8 / LN2))
        inverse = (TOP_CODE * jnp.exp(code * (-LN2 / 8)))[0:1]
        for u in range(8):
            k0, k1, k2, k3 = (acc_ref[u, pl.ds(k, 64, stride=4), :] for k in range(4))
            upper = jnp.where(even_group, k0, k1)
            lower = jnp.where(even_group, k2, k3)
            north.append(jnp.where(half, upper, pltpu.roll(lower, 64, 1)))
            south.append(jnp.where(half, pltpu.roll(upper, 64, 1), lower))
        at = first // 8 + step
        for hemi, part in enumerate((north, south)):
            base = hemi * 64 * ROWS
            for r in range(3):
                words = []
                for h in (0, 4):
                    row = jnp.where(spare, pltpu.roll(part[h + 3], 24 - 8 * r, 1), part[h + r])
                    words.append(jnp.round(row * inverse).astype(jnp.int32))
                out_ref[pl.ds(base + 3 * at + r, 64, stride=ROWS), :] = (words[0] & 0xFFFF) | (words[1] << 16)
            scales = out_ref[pl.ds(base + 9, 64, stride=ROWS), :]
            code_row = jnp.broadcast_to(code[0:1].astype(jnp.int32), (64, 128))
            out_ref[pl.ds(base + 9, 64, stride=ROWS), :] = jnp.where(lane == at, code_row, scales)
        return carry

    lax.fori_loop(0, count // 8, octet, 0)


def legendre_call(first, count, orders, coefs, legendre, before=None):
    smem, vmem = pl.BlockSpec(memory_space=pltpu.SMEM), pl.BlockSpec(memory_space=pltpu.VMEM)
    args = [orders, *coefs, legendre] + ([] if before is None else [before])
    return pl.pallas_call(
        functools.partial(legendre_kernel, first, count, before is not None),
        out_shape=jax.ShapeDtypeStruct((N_DEV * ROWS, 128), jnp.int32),
        in_specs=[smem] + [vmem] * (len(args) - 1),
        out_specs=vmem,
        scratch_shapes=[
            pltpu.VMEM((LB // 128, 2 * CH * count, 128), f32),
            pltpu.VMEM((8, 256, 128), f32),
        ],
        compiler_params=pltpu.CompilerParams(vmem_limit_bytes=VMEM_LEG),
        cost_estimate=pl.CostEstimate(flops=count * 256 * LB * 256, bytes_accessed=count * 256 * LB * 2, transcendentals=0),
    )(*args)


def map_kernel(
    orders_ref, lens_ref, data_ref, lane_len_ref, stage1_ref, twiddle_ref, stage2_ref, out_ref,
    slot_ref, place_ref, turned_ref, map_ref, low_ref, high_ref, hot_ref, cov_ref, comb_ref, final_ref,
):
    lane = lax.broadcasted_iota(jnp.int32, (N_DEV, 128), 1)
    which = (lane & 31) >> 3
    codes = data_ref[pl.ds(9, N_DEV, stride=ROWS), :].astype(f32)
    scales = jnp.exp(codes * (LN2 / 8)) * (1.0 / TOP_CODE)
    for octet in range(3):
        scale = scales[:, octet : octet + 1]
        words = [data_ref[pl.ds(3 * octet + r, N_DEV, stride=ROWS), :] for r in range(3)]
        for h in range(2):
            rolled = []
            for r in range(3):
                code = words[r] >> 16 if h else (words[r] << 16) >> 16
                value = code.astype(f32) * scale
                slot = 8 * octet + 4 * h + r
                slot_ref[slot * N_DEV : (slot + 1) * N_DEV, :] = value
                rolled.append(pltpu.roll(value, 128 - (24 - 8 * r), 1))
            slot = 8 * octet + 4 * h + 3
            value = jnp.where(which == 0, rolled[0], jnp.where(which == 1, rolled[1], rolled[2]))
            slot_ref[slot * N_DEV : (slot + 1) * N_DEV, :] = value

    def place(src, carry):
        base = ((src & (N_BLK - 1)) * N_CHAN + (src >> 5)) * NSLOT
        for slot in range(NSLOT):
            m = orders_ref[base + slot]
            place_ref[pl.ds(m, 1), :] = slot_ref[pl.ds(slot * N_DEV + src, 1), :]
        return carry

    lax.fori_loop(0, N_DEV, place, 0)
    place_ref[0:1, :] = place_ref[0:1, :] * 0.5

    for m2 in range(NM2):
        block = place_ref[m2 * 128 : (m2 + 1) * 128, :].T
        for k in range(NCYC):
            turned_ref[pl.ds(k * 2 * CH * NM2 + m2, 2 * CH, stride=NM2), :] = block[k * 32 : k * 32 + 24]

    stage1 = stage1_ref[...]

    def transform(i, carry):
        tc, ts = twiddle_ref[0:64, :], twiddle_ref[64:128, :]
        outer = []
        for pair in range(PAIRS):
            parts = []
            for j in range(2):
                start = pl.multiple_of((i * PAIRS + pair) * 96 + j * 48, 16)
                high, low = split2(turned_ref[pl.ds(start, 48), :])
                parts.append(jnp.concatenate([high, low, high], axis=0))
            inner = dot_nn(stage1, jnp.concatenate(parts, axis=1))
            for j in range(2):
                re, im = inner[0:64, j * 128 : (j + 1) * 128], inner[64:128, j * 128 : (j + 1) * 128]
                outer.append(jnp.concatenate([re * tc - im * ts, re * ts + im * tc], axis=1))
        high, low = split2(jnp.concatenate(outer, axis=0))
        both = dot_nn(high, stage2_ref[...])
        maps = both[:, 0:128] + (both[:, 128:256] + dot_nn(low, stage2_ref[:, 0:128]))
        map_ref[pl.ds(pl.multiple_of(i * PAIRS * 128, 128), PAIRS * 128), :] = maps
        return carry

    lax.fori_loop(0, NCYC * CH // (2 * PAIRS), transform, 0, unroll=4)

    chunk = lax.broadcasted_iota(jnp.int32, (64, 128), 1)
    offset = lax.broadcasted_iota(jnp.int32, (64, 128), 0)
    low_ref[...] = jnp.zeros_like(low_ref)
    high_ref[...] = jnp.zeros_like(high_ref)
    cov_ref[...] = jnp.zeros_like(cov_ref)

    def sectors(k):
        start = chunk * 64
        which = jnp.zeros((64, 128), jnp.int32)
        bound = jnp.full((64, 128), PIX, jnp.int32)
        end = jnp.int32(0)
        for q in range(NSEC):
            end = end + lens_ref[k, q]
            passed = end <= start
            which = which + passed.astype(jnp.int32)
            bound = jnp.minimum(bound, jnp.where(passed, PIX, end))
        return which, start + offset < bound

    def moments(k, carry):
        which, inside = sectors(k)
        row = lax.broadcasted_iota(jnp.int32, (64, 128), 0)
        own = (row >> 4) == k
        hot_low = (own & ((row & 15) == which)).astype(bf16)
        hot_high = (own & ((row & 15) == which + 1)).astype(bf16)
        hot_ref[pl.ds(pl.multiple_of(k * 128, 128), 64), :] = hot_low
        hot_ref[pl.ds(pl.multiple_of(k * 128 + 64, 64), 64), :] = hot_high
        base = pl.multiple_of(k * CH * 64, 64)
        for i in range(CH):
            value = map_ref[pl.ds(base + i * 64, 64), :]
            low = jnp.where(inside, value, 0.0)
            high = jnp.where(inside, 0.0, value)
            for j in range(i, CH):
                other = map_ref[pl.ds(base + j * 64, 64), :]
                for part, ref in ((low, low_ref), (high, high_ref)):
                    total = jnp.sum(part * other, axis=0, keepdims=True)
                    ref[i * 16 + j : i * 16 + j + 1, :] = total
                    if i != j:
                        ref[j * 16 + i : j * 16 + i + 1, :] = total
        total = cov_ref[...]
        for ref, hot in ((low_ref, hot_low), (high_ref, hot_high)):
            for part in split3(ref[...]):
                total = total + dot_nt(part, hot)
        cov_ref[...] = total
        return carry

    lax.fori_loop(0, NCYC, moments, 0)

    scale = 1.0 / lane_len_ref[...].astype(f32)
    sub = lax.broadcasted_iota(jnp.int32, (16, 64), 0)
    mat = [cov_ref[i * 16 : (i + 1) * 16, :] * scale for i in range(CH)]
    trace = mat[0][0:1]
    for i in range(1, CH):
        trace = trace + mat[i][i : i + 1]
    ridge = trace * (RIDGE_FACTOR / CH)
    for i in range(CH):
        mat[i] = jnp.where(sub == CH, 1.0, jnp.where(sub == i, mat[i] + ridge, mat[i]))
    for p in range(CH):
        pivot = mat[p] / mat[p][p : p + 1]
        for i in range(CH):
            mat[i] = pivot if i == p else mat[i] - mat[i][p : p + 1] * pivot
    solved = [mat[i][CH : CH + 1] for i in range(CH)]
    norm = solved[0]
    for i in range(1, CH):
        norm = norm + solved[i]
    weights = jnp.concatenate([s / norm for s in solved] + [jnp.zeros((4, 64), f32)], axis=0)
    weight_parts = split3(weights)

    def combine(k, carry):
        _, inside = sectors(k)
        chunk_weights = []
        for h in range(2):
            hot = hot_ref[pl.ds(pl.multiple_of(k * 128 + h * 64, 64), 64), :]
            chunk_weights.append(sum(dot_nn(part, hot) for part in weight_parts))
        base = pl.multiple_of(k * CH * 64, 64)
        total = jnp.zeros((64, 128), f32)
        for c in range(CH):
            weight = jnp.where(inside, chunk_weights[0][c : c + 1], chunk_weights[1][c : c + 1])
            total = total + weight * map_ref[pl.ds(base + c * 64, 64), :]
        wide = jnp.concatenate([total, total], axis=0).T
        comb_ref[...] = wide
        pair = jnp.where(chunk < 64, comb_ref[pl.ds(0, 64, stride=2), :], comb_ref[pl.ds(1, 64, stride=2), :])
        out_ref[k] = pair
        return carry

    lax.fori_loop(0, NCYC, combine, 0)


def map_call(orders, lens, data):
    stage1, twiddle, stage2 = tables()
    smem, vmem = pl.BlockSpec(memory_space=pltpu.SMEM), pl.BlockSpec(memory_space=pltpu.VMEM)
    return pl.pallas_call(
        map_kernel,
        out_shape=jax.ShapeDtypeStruct((NCYC, 64, 128), f32),
        in_specs=[smem, smem] + [vmem] * 5,
        out_specs=vmem,
        scratch_shapes=[
            pltpu.VMEM((NSLOT * N_DEV, 128), f32),
            pltpu.VMEM((M, 128), f32),
            pltpu.VMEM((NCYC * 2 * CH * NM2, 128), f32),
            pltpu.VMEM((NCYC * CH * 64, 128), f32),
            pltpu.VMEM((CH * 16, 128), f32),
            pltpu.VMEM((CH * 16, 128), f32),
            pltpu.VMEM((NCYC * 128, 128), bf16),
            pltpu.VMEM((CH * 16, 64), f32),
            pltpu.VMEM((128, 128), f32),
            pltpu.VMEM((8, 128), f32),
        ],
        compiler_params=pltpu.CompilerParams(vmem_limit_bytes=40 * 2**20),
    )(orders, lens, data, lens.reshape(1, NCYC * NSEC), stage1, twiddle, stage2)


def exchange(coeffs, first, count, me):
    part = coeffs.reshape(6, N_CHAN, NSLOT, LB)[:, :, first : first + count]
    pieces = {}
    for k in (0, 2, 1, 3):
        piece = lax.dynamic_index_in_dim(part, (me + k) & (N_CHAN - 1), 1, keepdims=False)
        if k:
            piece = lax.ppermute(piece, "chan", [(i, (i + k) % N_CHAN) for i in range(N_CHAN)])
        pieces[k] = piece
    return [pieces[k] for k in range(N_CHAN)]


def per_device(coeffs, legendre, m_order, sector_len):
    me = lax.axis_index("chan")
    sent, first = None, 0
    pieces = []
    for count in CHUNKS:
        pieces.append((first, count, exchange(coeffs, first, count, me)))
        first += count
    legendre = fetch_call(legendre[0])
    for first, count, piece in pieces:
        sent = legendre_call(first, count, m_order, piece, legendre, sent)
    data = lax.all_to_all(sent.reshape(N_DEV, 1, ROWS * 128), ("chan", "blk"), 0, 0, tiled=True)
    out = map_call(m_order, sector_len, data.reshape(N_DEV * ROWS, 128))
    return out.reshape(NCYC, PIX)


def solution(mesh):
    placed = (
        P("chan", None, "blk", None),
        P("chan", "blk", None, None),
        P(),
        P(("chan", "blk"), None),
    )
    return jax.shard_map(
        per_device, mesh=mesh, in_specs=placed, out_specs=P(("chan", "blk"), None), check_vma=False
    )
```

```python
import functools

import jax
import jax.numpy as jnp
import ml_dtypes
import numpy as np
from jax import lax
from jax.experimental import pallas as pl
from jax.experimental.pallas import tpu as pltpu
from jax.sharding import PartitionSpec as P

M = 3072
LB = 1536
PIX = 8192
CH = 12
NSEC = 16
NSLOT = 24
NCYC = 4
N_CHAN = 4
N_BLK = 32
N_DEV = N_CHAN * N_BLK
RIDGE_FACTOR = 0.05

NA, NB, NM1, NM2 = 128, 64, 128, 24
PAIRS = 6
ROWS = 10

CHUNKS = (16, 8)
VMEM_LEG = 16 * 2**20
FETCHES = 6
MOMENTS_UNROLL = 4
TOP_CODE = 32000.0
LN2 = float(np.log(2.0))

f32, bf16 = jnp.float32, jnp.bfloat16


def split_np(x):
    high = x.astype(ml_dtypes.bfloat16)
    low = (x - high.astype(np.float64)).astype(ml_dtypes.bfloat16)
    return high, low


@functools.cache
def tables():
    b, m2 = np.arange(NB)[:, None], np.arange(NM2)[None, :]
    angle = 2 * np.pi * ((b * m2) % 64) / 64
    stage1 = np.block([[np.cos(angle), -np.sin(angle)], [np.sin(angle), np.cos(angle)]])
    high, low = split_np(stage1)
    stage1 = np.concatenate([high, high, low], axis=1)
    m1 = np.arange(NM1)[None, :]
    angle = 2 * np.pi * b * m1 / PIX
    twiddle = np.concatenate([np.cos(angle), np.sin(angle)], axis=0).astype(np.float32)
    m1, a = np.arange(NM1)[:, None], np.arange(NA)[None, :]
    angle = 2 * np.pi * ((m1 * a) % 128) / 128
    stage2 = 2.0 * np.concatenate([np.cos(angle), -np.sin(angle)], axis=0)
    stage2 = np.concatenate(split_np(stage2), axis=1)
    return stage1, twiddle, stage2


def split2(x):
    high = x.astype(bf16)
    return high, (x - high.astype(f32)).astype(bf16)


def split3(x):
    high = x.astype(bf16)
    rest = x - high.astype(f32)
    mid = rest.astype(bf16)
    return high, mid, (rest - mid.astype(f32)).astype(bf16)


def dot_nn(x, y):
    return lax.dot_general(x, y, (((1,), (0,)), ((), ())), preferred_element_type=f32)


def dot_nt(x, y):
    return lax.dot_general(x, y, (((1,), (1,)), ((), ())), preferred_element_type=f32)


def fetch_kernel(source_ref, out_ref, sems):
    step = NSLOT // FETCHES
    copies = [
        pltpu.make_async_copy(source_ref.at[pl.ds(i * step, step)], out_ref.at[pl.ds(i * step, step)], sems.at[i])
        for i in range(FETCHES)
    ]
    for copy in copies:
        copy.start()
    for copy in copies:
        copy.wait()


def fetch_call(legendre):
    return pl.pallas_call(
        fetch_kernel,
        out_shape=jax.ShapeDtypeStruct(legendre.shape, legendre.dtype),
        in_specs=[pl.BlockSpec(memory_space=pl.ANY)],
        out_specs=pl.BlockSpec(memory_space=pltpu.VMEM),
        scratch_shapes=[pltpu.SemaphoreType.DMA((FETCHES,))],
        compiler_params=pltpu.CompilerParams(vmem_limit_bytes=VMEM_LEG),
        cost_estimate=pl.CostEstimate(flops=0, bytes_accessed=2 * legendre.size * 2, transcendentals=0),
    )(legendre)


def legendre_kernel(first, count, has_before, orders_ref, *refs):
    coef_refs, refs = refs[:4], refs[4:]
    leg_ref, refs = refs[0], refs[1:]
    before_ref, refs = (refs[0], refs[1:]) if has_before else (None, refs)
    out_ref, wide_ref, acc_ref = refs

    me = lax.axis_index("chan")
    own = (lax.axis_index("blk") * N_CHAN + me) * NSLOT + first

    for k in range(4):
        source = (me - k) & (N_CHAN - 1)
        for i in range(6):
            value = coef_refs[k][i].astype(f32)
            start = pl.multiple_of((source * 6 + i) * count, 8)
            for j in range(LB // 128):
                wide_ref[j, pl.ds(start, count), :] = value[:, j * 128 : (j + 1) * 128]
    if has_before:
        out_ref[...] = before_ref[...]
    else:
        out_ref[...] = jnp.zeros_like(out_ref)

    degree = (M - LB) + lax.broadcasted_iota(jnp.int32, (1, LB), 1)
    lane = lax.broadcasted_iota(jnp.int32, (64, 128), 1)
    half = lane < 64
    even_group = (lane & 32) == 0
    spare = (lane & 31) >= 24

    def octet(step, carry):
        slots = []
        for pair in range(4):
            slot = step * 8 + pair * 2
            swap = (orders_ref[own + slot] >= M // 2).astype(jnp.int32)
            slots += [slot + swap, slot + 1 - swap]
        for u, slot in enumerate(slots):
            m = orders_ref[own + slot]
            coef = jnp.concatenate(
                [wide_ref[j, pl.ds(slot, 2 * CH, stride=count), :] for j in range(LB // 128)], axis=1
            )
            keep = (degree >= m).astype(f32)
            sign = (1 - 2 * ((degree + m) & 1)).astype(f32) * keep
            none = jnp.zeros((8, LB), f32)
            up = jnp.concatenate([coef * keep, none], axis=0).astype(bf16)
            down = jnp.concatenate([coef * sign, none], axis=0).astype(bf16)
            rhs = jnp.concatenate([up, up, down, down], axis=0)
            acc_ref[u] = dot_nt(leg_ref[first + slot], rhs)
        top = jnp.maximum(jnp.abs(acc_ref[0]), jnp.abs(acc_ref[1]))
        for u in range(2, 8):
            top = jnp.maximum(top, jnp.abs(acc_ref[u]))
        top = jnp.max(jnp.max(top, axis=0, keepdims=True), axis=1, keepdims=True)
        top = jnp.broadcast_to(jnp.maximum(top, 1e-30), (8, 128))
        code = jnp.ceil(jnp.log(top) * (8 / LN2))
        inverse = (TOP_CODE * jnp.exp(code * (-LN2 / 8)))[0:1]
        north, south = [], []
        for pair in range(4):
            words = []
            for u in (2 * pair, 2 * pair + 1):
                k0, k1, k2, k3 = (acc_ref[u, pl.ds(k, 64, stride=4), :] for k in range(4))
                upper = jnp.round(jnp.where(even_group, k0, k1) * inverse).astype(jnp.int32)
                lower = jnp.round(jnp.where(even_group, k2, k3) * inverse).astype(jnp.int32)
                words.append((upper & 0xFFFF) | (lower << 16))
            north.append(jnp.where(half, words[0], pltpu.roll(words[1], 64, 1)))
            south.append(jnp.where(half, pltpu.roll(words[0], 64, 1), words[1]))
        at = first // 8 + step
        code_row = jnp.broadcast_to(code[0:1].astype(jnp.int32), (64, 128))
        for hemi, part in enumerate((north, south)):
            base = hemi * 64 * ROWS
            for r in range(3):
                row = jnp.where(spare, pltpu.roll(part[3], 24 - 8 * r, 1), part[r])
                out_ref[pl.ds(base + 3 * at + r, 64, stride=ROWS), :] = row
            scales = out_ref[pl.ds(base + 9, 64, stride=ROWS), :]
            out_ref[pl.ds(base + 9, 64, stride=ROWS), :] = jnp.where(lane == at, code_row, scales)
        return carry

    lax.fori_loop(0, count // 8, octet, 0)


def legendre_call(first, count, orders, coefs, legendre, before=None):
    smem, vmem = pl.BlockSpec(memory_space=pltpu.SMEM), pl.BlockSpec(memory_space=pltpu.VMEM)
    args = [orders, *coefs, legendre] + ([] if before is None else [before])
    return pl.pallas_call(
        functools.partial(legendre_kernel, first, count, before is not None),
        out_shape=jax.ShapeDtypeStruct((N_DEV * ROWS, 128), jnp.int32),
        in_specs=[smem] + [vmem] * (len(args) - 1),
        out_specs=vmem,
        scratch_shapes=[
            pltpu.VMEM((LB // 128, 2 * CH * count, 128), f32),
            pltpu.VMEM((8, 256, 128), f32),
        ],
        compiler_params=pltpu.CompilerParams(vmem_limit_bytes=VMEM_LEG),
        cost_estimate=pl.CostEstimate(flops=count * 256 * LB * 256, bytes_accessed=count * 256 * LB * 2, transcendentals=0),
    )(*args)


def map_kernel(
    orders_ref, lens_ref, data_ref, lane_len_ref, stage1_ref, twiddle_ref, stage2_ref, out_ref,
    pair_ref, place_ref, turned_ref, map_ref, part_ref, sums_ref, bound_ref, hot_ref, cov_ref, spread_ref, comb_ref, final_ref,
):
    lane = lax.broadcasted_iota(jnp.int32, (N_DEV, 128), 1)
    which = (lane & 31) >> 3
    scales = data_ref[pl.ds(9, N_DEV, stride=ROWS), :]
    for octet in range(3):
        scale = jnp.broadcast_to(scales[:, octet : octet + 1], (N_DEV, 128))
        words = [data_ref[pl.ds(3 * octet + r, N_DEV, stride=ROWS), :] for r in range(3)]
        rolled = [pltpu.roll(words[r], 128 - (24 - 8 * r), 1) for r in range(3)]
        words.append(jnp.where(which == 0, rolled[0], jnp.where(which == 1, rolled[1], rolled[2])))
        for r in range(4):
            pair = 4 * octet + r
            pair_ref[pair * N_DEV : (pair + 1) * N_DEV, :] = jnp.where(which == 3, scale, words[r])

    def place(src, carry):
        base = ((src & (N_BLK - 1)) * N_CHAN + (src >> 5)) * NSLOT
        for pair in range(NSLOT // 2):
            m = orders_ref[base + 2 * pair]
            row = pair_ref[pl.ds(pair * N_DEV + src, 1), :]
            place_ref[pl.ds(m, 1), :] = row
            place_ref[pl.ds(M - 1 - m, 1), :] = row
        return carry

    lax.fori_loop(0, N_DEV, place, 0, unroll=2)

    for m2 in range(NM2):
        block = place_ref[m2 * 128 : (m2 + 1) * 128, :].T
        side = 64 * (m2 // (NM2 // 2))
        scale = jnp.exp(block[side + 24 : side + 25].astype(f32) * (LN2 / 8)) * (1.0 / TOP_CODE)
        if m2 == 0:
            scale = jnp.where(lax.broadcasted_iota(jnp.int32, (1, 128), 1) == 0, 0.5 * scale, scale)
        for k in range(2):
            word = block[side + k * 32 : side + k * 32 + 24]
            for h, code in enumerate(((word << 16) >> 16, word >> 16)):
                start = (k + 2 * h) * 2 * CH * NM2 + m2
                turned_ref[pl.ds(start, 2 * CH, stride=NM2), :] = code.astype(f32) * scale

    stage1 = stage1_ref[...]

    def transform(i, carry):
        tc, ts = twiddle_ref[0:64, :], twiddle_ref[64:128, :]
        outer = []
        for pair in range(PAIRS):
            parts = []
            for j in range(2):
                start = pl.multiple_of((i * PAIRS + pair) * 96 + j * 48, 16)
                high, low = split2(turned_ref[pl.ds(start, 48), :])
                parts.append(jnp.concatenate([high, low, high], axis=0))
            inner = dot_nn(stage1, jnp.concatenate(parts, axis=1))
            for j in range(2):
                re, im = inner[0:64, j * 128 : (j + 1) * 128], inner[64:128, j * 128 : (j + 1) * 128]
                outer.append(jnp.concatenate([re * tc - im * ts, re * ts + im * tc], axis=1))
        high, low = split2(jnp.concatenate(outer, axis=0))
        both = dot_nn(high, stage2_ref[...])
        maps = both[:, 0:128] + (both[:, 128:256] + dot_nn(low, stage2_ref[:, 0:128]))
        map_ref[pl.ds(pl.multiple_of(i * PAIRS * 128, 128), PAIRS * 128), :] = maps
        return carry

    lax.fori_loop(0, NCYC * CH // (2 * PAIRS), transform, 0, unroll=4)

    chunk = lax.broadcasted_iota(jnp.int32, (64, 128), 1)
    offset = lax.broadcasted_iota(jnp.int32, (64, 128), 0)
    part_ref[...] = jnp.zeros_like(part_ref)

    hot_row = lax.broadcasted_iota(jnp.int32, (64, 128), 0)
    for k in range(NCYC):
        start = lax.broadcasted_iota(jnp.int32, (8, 128), 1) * 64
        which = jnp.zeros((8, 128), jnp.int32)
        bound = jnp.full((8, 128), PIX, jnp.int32)
        end = jnp.int32(0)
        for q in range(NSEC):
            end = end + lens_ref[k, q]
            passed = end <= start
            which = which + passed.astype(jnp.int32)
            bound = jnp.minimum(bound, jnp.where(passed, PIX, end))
        bound_ref[k * 8 : k * 8 + 8, :] = bound - start
        for h in range(2):
            hot = ((hot_row >> 4) == k) & ((hot_row & 15) == which[0:1] + h)
            hot_ref[:, (k * 2 + h) * 128 : (k * 2 + h + 1) * 128] = hot.astype(bf16)

    def moments(k, carry):
        inside = offset < bound_ref[pl.ds(pl.multiple_of(k * 8, 8), 1), :]
        base = pl.multiple_of(k * CH * 64, 64)
        for i in range(CH):
            value = map_ref[pl.ds(base + i * 64, 64), :]
            low = jnp.where(inside, value, 0.0)
            high = jnp.where(inside, 0.0, value)
            for j in range(i, CH):
                other = map_ref[pl.ds(base + j * 64, 64), :]
                for h, part in enumerate((low, high)):
                    product = part * other
                    pairs = [product[b * 16 : b * 16 + 8] + product[b * 16 + 8 : b * 16 + 16] for b in range(4)]
                    at = (h * CH + i) * 128 + j * 8
                    part_ref[at : at + 8, :] = (pairs[0] + pairs[1]) + (pairs[2] + pairs[3])
        for h in range(2):
            for i in range(CH):
                at = (h * CH + i) * 128
                summed = [part_ref[pl.ds(at + b, 16, stride=8), :] for b in range(8)]
                while len(summed) > 1:
                    summed = [summed[b] + summed[b + 1] for b in range(0, len(summed), 2)]
                sums_ref[pl.ds(pl.multiple_of((k * 2 + h) * CH * 16, 16) + i * 16, 16), :] = summed[0]
        return carry

    lax.fori_loop(0, NCYC, moments, 0, unroll=MOMENTS_UNROLL)
    sums = jnp.concatenate([sums_ref[g * CH * 16 : (g + 1) * CH * 16, :] for g in range(2 * NCYC)], axis=1)
    total = None
    for part in split3(sums):
        product = dot_nt(part, hot_ref[...])
        total = product if total is None else total + product
    cov_ref[...] = total
    for i in range(CH):
        for j in range(i + 1, CH):
            cov_ref[j * 16 + i : j * 16 + i + 1, :] = cov_ref[i * 16 + j : i * 16 + j + 1, :]

    scale = 1.0 / lane_len_ref[...].astype(f32)
    sub = lax.broadcasted_iota(jnp.int32, (16, 64), 0)
    mat = [cov_ref[i * 16 : (i + 1) * 16, :] * scale for i in range(CH)]
    trace = mat[0][0:1]
    for i in range(1, CH):
        trace = trace + mat[i][i : i + 1]
    ridge = trace * (RIDGE_FACTOR / CH)
    for i in range(CH):
        mat[i] = jnp.where(sub == CH, 1.0, jnp.where(sub == i, mat[i] + ridge, mat[i]))
    for p in range(CH):
        pivot = mat[p] / mat[p][p : p + 1]
        for i in range(CH):
            mat[i] = pivot if i == p else mat[i] - mat[i][p : p + 1] * pivot
    solved = [mat[i][CH : CH + 1] for i in range(CH)]
    norm = solved[0]
    for i in range(1, CH):
        norm = norm + solved[i]
    weights = jnp.concatenate([s / norm for s in solved] + [jnp.zeros((4, 64), f32)], axis=0)
    spread = dot_nn(jnp.concatenate(split3(weights), axis=0), hot_ref[...])
    spread = spread[0:16] + (spread[16:32] + spread[32:48])
    for g in range(2 * NCYC):
        spread_ref[g * 16 : (g + 1) * 16, :] = spread[:, g * 128 : (g + 1) * 128]

    def combine(k, carry):
        inside = offset < bound_ref[pl.ds(pl.multiple_of(k * 8, 8), 1), :]
        chunk_weights = [spread_ref[pl.ds(pl.multiple_of((k * 2 + h) * 16, 16), 16), :] for h in range(2)]
        base = pl.multiple_of(k * CH * 64, 64)
        total = jnp.zeros((64, 128), f32)
        for c in range(CH):
            weight = jnp.where(inside, chunk_weights[0][c : c + 1], chunk_weights[1][c : c + 1])
            total = total + weight * map_ref[pl.ds(base + c * 64, 64), :]
        wide = jnp.concatenate([total, total], axis=0).T
        comb_ref[k] = wide
        pair = jnp.where(chunk < 64, comb_ref[k, pl.ds(0, 64, stride=2), :], comb_ref[k, pl.ds(1, 64, stride=2), :])
        final_ref[pl.ds(k, 64, stride=NCYC), :] = pair
        return carry

    lax.fori_loop(0, NCYC, combine, 0, unroll=4)
    for i in range(64):
        out_ref[:, i * 128 : (i + 1) * 128] = final_ref[i * NCYC : (i + 1) * NCYC, :]


def map_call(orders, lens, data):
    stage1, twiddle, stage2 = tables()
    smem, vmem = pl.BlockSpec(memory_space=pltpu.SMEM), pl.BlockSpec(memory_space=pltpu.VMEM)
    return pl.pallas_call(
        map_kernel,
        out_shape=jax.ShapeDtypeStruct((NCYC, PIX), f32),
        in_specs=[smem, smem] + [vmem] * 5,
        out_specs=vmem,
        scratch_shapes=[
            pltpu.VMEM((NSLOT // 2 * N_DEV, 128), jnp.int32),
            pltpu.VMEM((M, 128), jnp.int32),
            pltpu.VMEM((NCYC * 2 * CH * NM2, 128), f32),
            pltpu.VMEM((NCYC * CH * 64, 128), f32),
            pltpu.VMEM((2 * CH * 128, 128), f32),
            pltpu.VMEM((2 * NCYC * CH * 16, 128), f32),
            pltpu.VMEM((NCYC * 8, 128), jnp.int32),
            pltpu.VMEM((64, 2 * NCYC * 128), bf16),
            pltpu.VMEM((CH * 16, 64), f32),
            pltpu.VMEM((2 * NCYC * 16, 128), f32),
            pltpu.VMEM((NCYC, 128, 128), f32),
            pltpu.VMEM((64 * NCYC, 128), f32),
        ],
        compiler_params=pltpu.CompilerParams(vmem_limit_bytes=40 * 2**20),
    )(orders, lens, data, lens.reshape(1, NCYC * NSEC), stage1, twiddle, stage2)


def slices_kernel(coef_ref, *refs):
    outs, sems = refs[:-1], refs[-1]
    me = lax.axis_index("chan")
    copies, first = [], 0
    for n, count in enumerate(CHUNKS):
        for k in (2, 1, 3, 0):
            source = coef_ref.at[:, (me + k) & (N_CHAN - 1), pl.ds(first, count)]
            copies.append(pltpu.make_async_copy(source, outs[n * N_CHAN + k], sems.at[n * N_CHAN + k]))
        first += count
    for copy in copies:
        copy.start()
    for copy in copies:
        copy.wait()


def exchange(coeffs):
    shapes = [jax.ShapeDtypeStruct((6, count, LB), bf16) for count in CHUNKS for _ in range(N_CHAN)]
    pieces = pl.pallas_call(
        slices_kernel,
        out_shape=shapes,
        in_specs=[pl.BlockSpec(memory_space=pl.ANY)],
        out_specs=[pl.BlockSpec(memory_space=pltpu.VMEM)] * len(shapes),
        scratch_shapes=[pltpu.SemaphoreType.DMA((len(shapes),))],
        compiler_params=pltpu.CompilerParams(vmem_limit_bytes=VMEM_LEG),
    )(coeffs.reshape(6, N_CHAN, NSLOT, LB))
    pieces = list(pieces)
    for n in range(len(CHUNKS)):
        for k in (2, 1, 3):
            at = n * N_CHAN + k
            pieces[at] = lax.ppermute(pieces[at], "chan", [(i, (i + k) % N_CHAN) for i in range(N_CHAN)])
    return [pieces[n * N_CHAN : (n + 1) * N_CHAN] for n in range(len(CHUNKS))]


def per_device(coeffs, legendre, m_order, sector_len):
    pieces = exchange(coeffs)
    legendre = fetch_call(legendre[0])
    sent, first = None, 0
    for count, piece in zip(CHUNKS, pieces):
        sent = legendre_call(first, count, m_order, piece, legendre, sent)
        first += count
    data = lax.all_to_all(sent.reshape(N_DEV, 1, ROWS * 128), ("chan", "blk"), 0, 0, tiled=True)
    return map_call(m_order, sector_len, data.reshape(N_DEV * ROWS, 128))


def solution(mesh):
    placed = (
        P("chan", None, "blk", None),
        P("chan", "blk", None, None),
        P(),
        P(("chan", "blk"), None),
    )
    return jax.shard_map(
        per_device, mesh=mesh, in_specs=placed, out_specs=P(("chan", "blk"), None), check_vma=False
    )
```

```python
import functools

import jax
import jax.numpy as jnp
import ml_dtypes
import numpy as np
from jax import lax
from jax.experimental import pallas as pl
from jax.experimental.pallas import tpu as pltpu
from jax.sharding import PartitionSpec as P

M = 3072
LB = 1536
PIX = 8192
CH = 12
NSEC = 16
NSLOT = 24
NCYC = 4
N_CHAN = 4
N_BLK = 32
N_DEV = N_CHAN * N_BLK
RIDGE_FACTOR = 0.05

NA, NB, NM1, NM2 = 128, 64, 128, 24
PAIRS = 6
ROWS = 10

CHUNKS = (16, 8)
VMEM_LEG = 16 * 2**20
FETCHES = 6
ORDER = (2, 1, 3)
MOMENTS_UNROLL = 4
TOP_CODE = 32000.0
LN2 = float(np.log(2.0))

f32, bf16 = jnp.float32, jnp.bfloat16


def split_np(x):
    high = x.astype(ml_dtypes.bfloat16)
    low = (x - high.astype(np.float64)).astype(ml_dtypes.bfloat16)
    return high, low


@functools.cache
def tables():
    b, m2 = np.arange(NB)[:, None], np.arange(NM2)[None, :]
    angle = 2 * np.pi * ((b * m2) % 64) / 64
    stage1 = np.block([[np.cos(angle), -np.sin(angle)], [np.sin(angle), np.cos(angle)]])
    high, low = split_np(stage1)
    stage1 = np.concatenate([high, high, low], axis=1)
    m1 = np.arange(NM1)[None, :]
    angle = 2 * np.pi * b * m1 / PIX
    twiddle = np.concatenate([np.cos(angle), np.sin(angle)], axis=0).astype(np.float32)
    m1, a = np.arange(NM1)[:, None], np.arange(NA)[None, :]
    angle = 2 * np.pi * ((m1 * a) % 128) / 128
    stage2 = 2.0 * np.concatenate([np.cos(angle), -np.sin(angle)], axis=0)
    stage2 = np.concatenate(split_np(stage2), axis=1)
    return stage1, twiddle, stage2


def split2(x):
    high = x.astype(bf16)
    return high, (x - high.astype(f32)).astype(bf16)


def split3(x):
    high = x.astype(bf16)
    rest = x - high.astype(f32)
    mid = rest.astype(bf16)
    return high, mid, (rest - mid.astype(f32)).astype(bf16)


def dot_nn(x, y):
    return lax.dot_general(x, y, (((1,), (0,)), ((), ())), preferred_element_type=f32)


def dot_nt(x, y):
    return lax.dot_general(x, y, (((1,), (1,)), ((), ())), preferred_element_type=f32)


def fetch_kernel(source_ref, out_ref, sems):
    step = NSLOT // FETCHES
    copies = [
        pltpu.make_async_copy(source_ref.at[pl.ds(i * step, step)], out_ref.at[pl.ds(i * step, step)], sems.at[i])
        for i in range(FETCHES)
    ]
    for copy in copies:
        copy.start()
    for copy in copies:
        copy.wait()


def fetch_call(legendre):
    return pl.pallas_call(
        fetch_kernel,
        out_shape=jax.ShapeDtypeStruct(legendre.shape, legendre.dtype),
        in_specs=[pl.BlockSpec(memory_space=pl.ANY)],
        out_specs=pl.BlockSpec(memory_space=pltpu.VMEM),
        scratch_shapes=[pltpu.SemaphoreType.DMA((FETCHES,))],
        compiler_params=pltpu.CompilerParams(vmem_limit_bytes=VMEM_LEG),
        cost_estimate=pl.CostEstimate(flops=0, bytes_accessed=2 * legendre.size * 2, transcendentals=0),
    )(legendre)


def legendre_kernel(first, count, has_before, orders_ref, *refs):
    coef_refs, refs = refs[:4], refs[4:]
    leg_ref, refs = refs[0], refs[1:]
    before_ref, refs = (refs[0], refs[1:]) if has_before else (None, refs)
    out_ref, wide_ref, acc_ref = refs

    me = lax.axis_index("chan")
    own = (lax.axis_index("blk") * N_CHAN + me) * NSLOT + first

    for k in range(4):
        source = (me - k) & (N_CHAN - 1)
        for i in range(6):
            value = coef_refs[k][i].astype(f32)
            start = pl.multiple_of((source * 6 + i) * count, 8)
            for j in range(LB // 128):
                wide_ref[j, pl.ds(start, count), :] = value[:, j * 128 : (j + 1) * 128]
    if has_before:
        out_ref[...] = before_ref[...]
    else:
        out_ref[...] = jnp.zeros_like(out_ref)

    degree = (M - LB) + lax.broadcasted_iota(jnp.int32, (1, LB), 1)
    lane = lax.broadcasted_iota(jnp.int32, (64, 128), 1)
    half = lane < 64
    even_group = (lane & 32) == 0
    spare = (lane & 31) >= 24

    def octet(step, carry):
        at = first // 8 + step
        north, south = [], []
        code_row = jnp.zeros((8, 128), jnp.int32)
        for pair in range(4):
            slot = step * 8 + pair * 2
            swap = (orders_ref[own + slot] >= M // 2).astype(jnp.int32)
            top = None
            for u, slot in ((2 * pair, slot + swap), (2 * pair + 1, slot + 1 - swap)):
                m = orders_ref[own + slot]
                coef = jnp.concatenate(
                    [wide_ref[j, pl.ds(slot, 2 * CH, stride=count), :] for j in range(LB // 128)], axis=1
                )
                keep = (degree >= m).astype(f32)
                sign = (1 - 2 * ((degree + m) & 1)).astype(f32) * keep
                none = jnp.zeros((8, LB), f32)
                up = jnp.concatenate([coef * keep, none], axis=0).astype(bf16)
                down = jnp.concatenate([coef * sign, none], axis=0).astype(bf16)
                rhs = jnp.concatenate([up, up, down, down], axis=0)
                product = dot_nt(leg_ref[first + slot], rhs)
                acc_ref[u] = product
                most = jnp.max(jnp.abs(product), axis=0, keepdims=True)
                top = most if top is None else jnp.maximum(top, most)
            top = jnp.max(jnp.broadcast_to(top, (8, 128)), axis=1, keepdims=True)
            code = jnp.ceil(jnp.log(jnp.broadcast_to(jnp.maximum(top, 1e-30), (8, 128))) * (8 / LN2))
            inverse = (TOP_CODE * jnp.exp(code * (-LN2 / 8)))[0:1]
            code_row = jnp.where(lane[0:8] == 4 * at + pair, code.astype(jnp.int32), code_row)
            words = []
            for u in (2 * pair, 2 * pair + 1):
                k0, k1, k2, k3 = (acc_ref[u, pl.ds(k, 64, stride=4), :] for k in range(4))
                upper = jnp.round(jnp.where(even_group, k0, k1) * inverse).astype(jnp.int32)
                lower = jnp.round(jnp.where(even_group, k2, k3) * inverse).astype(jnp.int32)
                words.append((upper & 0xFFFF) | (lower << 16))
            north.append(jnp.where(half, words[0], pltpu.roll(words[1], 64, 1)))
            south.append(jnp.where(half, pltpu.roll(words[0], 64, 1), words[1]))
        code_row = jnp.broadcast_to(code_row[0:1], (64, 128))
        for hemi, part in enumerate((north, south)):
            base = hemi * 64 * ROWS
            for r in range(3):
                row = jnp.where(spare, pltpu.roll(part[3], 24 - 8 * r, 1), part[r])
                out_ref[pl.ds(base + 3 * at + r, 64, stride=ROWS), :] = row
            scales = out_ref[pl.ds(base + 9, 64, stride=ROWS), :]
            out_ref[pl.ds(base + 9, 64, stride=ROWS), :] = jnp.where((lane >> 2) == at, code_row, scales)
        return carry

    lax.fori_loop(0, count // 8, octet, 0, unroll=count // 8)


def legendre_call(first, count, orders, coefs, legendre, before=None):
    smem, vmem = pl.BlockSpec(memory_space=pltpu.SMEM), pl.BlockSpec(memory_space=pltpu.VMEM)
    args = [orders, *coefs, legendre] + ([] if before is None else [before])
    return pl.pallas_call(
        functools.partial(legendre_kernel, first, count, before is not None),
        out_shape=jax.ShapeDtypeStruct((N_DEV * ROWS, 128), jnp.int32),
        in_specs=[smem] + [vmem] * (len(args) - 1),
        out_specs=vmem,
        scratch_shapes=[
            pltpu.VMEM((LB // 128, 2 * CH * count, 128), f32),
            pltpu.VMEM((8, 256, 128), f32),
        ],
        compiler_params=pltpu.CompilerParams(vmem_limit_bytes=VMEM_LEG),
        cost_estimate=pl.CostEstimate(flops=count * 256 * LB * 256, bytes_accessed=count * 256 * LB * 2, transcendentals=0),
    )(*args)


def map_kernel(
    orders_ref, lens_ref, data_ref, lane_len_ref, stage1_ref, twiddle_ref, stage2_ref, out_ref,
    pair_ref, place_ref, turned_ref, map_ref, part_ref, sums_ref, bound_ref, hot_ref, cov_ref, spread_ref, comb_ref, final_ref,
):
    lane = lax.broadcasted_iota(jnp.int32, (N_DEV, 128), 1)
    which = (lane & 31) >> 3
    scales = data_ref[pl.ds(9, N_DEV, stride=ROWS), :]
    for octet in range(3):
        words = [data_ref[pl.ds(3 * octet + r, N_DEV, stride=ROWS), :] for r in range(3)]
        rolled = [pltpu.roll(words[r], 128 - (24 - 8 * r), 1) for r in range(3)]
        words.append(jnp.where(which == 0, rolled[0], jnp.where(which == 1, rolled[1], rolled[2])))
        for r in range(4):
            pair = 4 * octet + r
            scale = jnp.broadcast_to(scales[:, pair : pair + 1], (N_DEV, 128))
            pair_ref[pair * N_DEV : (pair + 1) * N_DEV, :] = jnp.where(which == 3, scale, words[r])

    def place(src, carry):
        base = ((src & (N_BLK - 1)) * N_CHAN + (src >> 5)) * NSLOT
        for pair in range(NSLOT // 2):
            m = orders_ref[base + 2 * pair]
            row = pair_ref[pl.ds(pair * N_DEV + src, 1), :]
            place_ref[pl.ds(m, 1), :] = row
            place_ref[pl.ds(M - 1 - m, 1), :] = row
        return carry

    lax.fori_loop(0, N_DEV, place, 0, unroll=2)

    for m2 in range(NM2):
        block = place_ref[m2 * 128 : (m2 + 1) * 128, :].T
        side = 64 * (m2 // (NM2 // 2))
        scale = jnp.exp(block[side + 24 : side + 25].astype(f32) * (LN2 / 8)) * (1.0 / TOP_CODE)
        if m2 == 0:
            scale = jnp.where(lax.broadcasted_iota(jnp.int32, (1, 128), 1) == 0, 0.5 * scale, scale)
        for k in range(2):
            word = block[side + k * 32 : side + k * 32 + 24]
            for h, code in enumerate(((word << 16) >> 16, word >> 16)):
                start = (k + 2 * h) * 2 * CH * NM2 + m2
                turned_ref[pl.ds(start, 2 * CH, stride=NM2), :] = code.astype(f32) * scale

    stage1 = stage1_ref[...]

    def transform(i, carry):
        tc, ts = twiddle_ref[0:64, :], twiddle_ref[64:128, :]
        outer = []
        for pair in range(PAIRS):
            parts = []
            for j in range(2):
                start = pl.multiple_of((i * PAIRS + pair) * 96 + j * 48, 16)
                high, low = split2(turned_ref[pl.ds(start, 48), :])
                parts.append(jnp.concatenate([high, low, high], axis=0))
            inner = dot_nn(stage1, jnp.concatenate(parts, axis=1))
            for j in range(2):
                re, im = inner[0:64, j * 128 : (j + 1) * 128], inner[64:128, j * 128 : (j + 1) * 128]
                outer.append(jnp.concatenate([re * tc - im * ts, re * ts + im * tc], axis=1))
        high, low = split2(jnp.concatenate(outer, axis=0))
        both = dot_nn(high, stage2_ref[...])
        maps = both[:, 0:128] + (both[:, 128:256] + dot_nn(low, stage2_ref[:, 0:128]))
        map_ref[pl.ds(pl.multiple_of(i * PAIRS * 128, 128), PAIRS * 128), :] = maps
        return carry

    lax.fori_loop(0, NCYC * CH // (2 * PAIRS), transform, 0, unroll=4)

    chunk = lax.broadcasted_iota(jnp.int32, (64, 128), 1)
    offset = lax.broadcasted_iota(jnp.int32, (64, 128), 0)
    part_ref[...] = jnp.zeros_like(part_ref)

    hot_row = lax.broadcasted_iota(jnp.int32, (64, 128), 0)
    for k in range(NCYC):
        start = lax.broadcasted_iota(jnp.int32, (8, 128), 1) * 64
        which = jnp.zeros((8, 128), jnp.int32)
        bound = jnp.full((8, 128), PIX, jnp.int32)
        end = jnp.int32(0)
        for q in range(NSEC):
            end = end + lens_ref[k, q]
            passed = end <= start
            which = which + passed.astype(jnp.int32)
            bound = jnp.minimum(bound, jnp.where(passed, PIX, end))
        bound_ref[k * 8 : k * 8 + 8, :] = bound - start
        for h in range(2):
            hot = ((hot_row >> 4) == k) & ((hot_row & 15) == which[0:1] + h)
            hot_ref[:, (k * 2 + h) * 128 : (k * 2 + h + 1) * 128] = hot.astype(bf16)

    def moments(k, carry):
        inside = offset < bound_ref[pl.ds(pl.multiple_of(k * 8, 8), 1), :]
        base = pl.multiple_of(k * CH * 64, 64)
        for i in range(CH):
            value = map_ref[pl.ds(base + i * 64, 64), :]
            low = jnp.where(inside, value, 0.0)
            high = jnp.where(inside, 0.0, value)
            for j in range(i, CH):
                other = map_ref[pl.ds(base + j * 64, 64), :]
                for h, part in enumerate((low, high)):
                    product = part * other
                    pairs = [product[b * 16 : b * 16 + 8] + product[b * 16 + 8 : b * 16 + 16] for b in range(4)]
                    at = (h * CH + i) * 128 + j * 8
                    part_ref[at : at + 8, :] = (pairs[0] + pairs[1]) + (pairs[2] + pairs[3])
        for h in range(2):
            for i in range(CH):
                at = (h * CH + i) * 128
                summed = [part_ref[pl.ds(at + b, 16, stride=8), :] for b in range(8)]
                while len(summed) > 1:
                    summed = [summed[b] + summed[b + 1] for b in range(0, len(summed), 2)]
                sums_ref[pl.ds(pl.multiple_of((k * 2 + h) * CH * 16, 16) + i * 16, 16), :] = summed[0]
        return carry

    lax.fori_loop(0, NCYC, moments, 0, unroll=MOMENTS_UNROLL)
    sums = jnp.concatenate([sums_ref[g * CH * 16 : (g + 1) * CH * 16, :] for g in range(2 * NCYC)], axis=1)
    total = None
    for part in split3(sums):
        product = dot_nt(part, hot_ref[...])
        total = product if total is None else total + product
    cov_ref[...] = total
    for i in range(CH):
        for j in range(i + 1, CH):
            cov_ref[j * 16 + i : j * 16 + i + 1, :] = cov_ref[i * 16 + j : i * 16 + j + 1, :]

    scale = 1.0 / lane_len_ref[...].astype(f32)
    sub = lax.broadcasted_iota(jnp.int32, (16, 64), 0)
    mat = [cov_ref[i * 16 : (i + 1) * 16, :] * scale for i in range(CH)]
    trace = mat[0][0:1]
    for i in range(1, CH):
        trace = trace + mat[i][i : i + 1]
    ridge = trace * (RIDGE_FACTOR / CH)
    for i in range(CH):
        mat[i] = jnp.where(sub == CH, 1.0, jnp.where(sub == i, mat[i] + ridge, mat[i]))
    for p in range(CH):
        pivot = mat[p] / mat[p][p : p + 1]
        for i in range(CH):
            mat[i] = pivot if i == p else mat[i] - mat[i][p : p + 1] * pivot
    solved = [mat[i][CH : CH + 1] for i in range(CH)]
    norm = solved[0]
    for i in range(1, CH):
        norm = norm + solved[i]
    weights = jnp.concatenate([s / norm for s in solved] + [jnp.zeros((4, 64), f32)], axis=0)
    spread = dot_nn(jnp.concatenate(split3(weights), axis=0), hot_ref[...])
    spread = spread[0:16] + (spread[16:32] + spread[32:48])
    for g in range(2 * NCYC):
        spread_ref[g * 16 : (g + 1) * 16, :] = spread[:, g * 128 : (g + 1) * 128]

    def combine(k, carry):
        inside = offset < bound_ref[pl.ds(pl.multiple_of(k * 8, 8), 1), :]
        chunk_weights = [spread_ref[pl.ds(pl.multiple_of((k * 2 + h) * 16, 16), 16), :] for h in range(2)]
        base = pl.multiple_of(k * CH * 64, 64)
        total = jnp.zeros((64, 128), f32)
        for c in range(CH):
            weight = jnp.where(inside, chunk_weights[0][c : c + 1], chunk_weights[1][c : c + 1])
            total = total + weight * map_ref[pl.ds(base + c * 64, 64), :]
        wide = jnp.concatenate([total, total], axis=0).T
        comb_ref[k] = wide
        pair = jnp.where(chunk < 64, comb_ref[k, pl.ds(0, 64, stride=2), :], comb_ref[k, pl.ds(1, 64, stride=2), :])
        final_ref[pl.ds(k, 64, stride=NCYC), :] = pair
        return carry

    lax.fori_loop(0, NCYC, combine, 0, unroll=4)
    for i in range(64):
        out_ref[:, i * 128 : (i + 1) * 128] = final_ref[i * NCYC : (i + 1) * NCYC, :]


def map_call(orders, lens, data):
    stage1, twiddle, stage2 = tables()
    smem, vmem = pl.BlockSpec(memory_space=pltpu.SMEM), pl.BlockSpec(memory_space=pltpu.VMEM)
    return pl.pallas_call(
        map_kernel,
        out_shape=jax.ShapeDtypeStruct((NCYC, PIX), f32),
        in_specs=[smem, smem] + [vmem] * 5,
        out_specs=vmem,
        scratch_shapes=[
            pltpu.VMEM((NSLOT // 2 * N_DEV, 128), jnp.int32),
            pltpu.VMEM((M, 128), jnp.int32),
            pltpu.VMEM((NCYC * 2 * CH * NM2, 128), f32),
            pltpu.VMEM((NCYC * CH * 64, 128), f32),
            pltpu.VMEM((2 * CH * 128, 128), f32),
            pltpu.VMEM((2 * NCYC * CH * 16, 128), f32),
            pltpu.VMEM((NCYC * 8, 128), jnp.int32),
            pltpu.VMEM((64, 2 * NCYC * 128), bf16),
            pltpu.VMEM((CH * 16, 64), f32),
            pltpu.VMEM((2 * NCYC * 16, 128), f32),
            pltpu.VMEM((NCYC, 128, 128), f32),
            pltpu.VMEM((64 * NCYC, 128), f32),
        ],
        compiler_params=pltpu.CompilerParams(vmem_limit_bytes=40 * 2**20),
    )(orders, lens, data, lens.reshape(1, NCYC * NSEC), stage1, twiddle, stage2)


def slices_kernel(coef_ref, *refs):
    outs, sems = refs[:-1], refs[-1]
    me = lax.axis_index("chan")
    copies, first = [], 0
    for n, count in enumerate(CHUNKS):
        for k in (2, 1, 3, 0):
            source = coef_ref.at[:, (me + k) & (N_CHAN - 1), pl.ds(first, count)]
            copies.append(pltpu.make_async_copy(source, outs[n * N_CHAN + k], sems.at[n * N_CHAN + k]))
        first += count
    for copy in copies:
        copy.start()
    for copy in copies:
        copy.wait()


def cut(coeffs):
    shapes = [jax.ShapeDtypeStruct((6, count, LB), bf16) for count in CHUNKS for _ in range(N_CHAN)]
    pieces = pl.pallas_call(
        slices_kernel,
        out_shape=shapes,
        in_specs=[pl.BlockSpec(memory_space=pl.ANY)],
        out_specs=[pl.BlockSpec(memory_space=pltpu.VMEM)] * len(shapes),
        scratch_shapes=[pltpu.SemaphoreType.DMA((len(shapes),))],
        compiler_params=pltpu.CompilerParams(vmem_limit_bytes=VMEM_LEG),
    )(coeffs.reshape(6, N_CHAN, NSLOT, LB))
    return [list(pieces[n * N_CHAN : (n + 1) * N_CHAN]) for n in range(len(CHUNKS))]


def send(pieces):
    pieces = list(pieces)
    for k in ORDER:
        pieces[k] = lax.ppermute(pieces[k], "chan", [(i, (i + k) % N_CHAN) for i in range(N_CHAN)])
    return pieces


def per_device(coeffs, legendre, m_order, sector_len):
    early, late = cut(coeffs)
    early = send(early)
    legendre, late = lax.optimization_barrier((fetch_call(legendre[0]), late))
    pieces = [early, send(late)]
    sent, first = None, 0
    for count, piece in zip(CHUNKS, pieces):
        sent = legendre_call(first, count, m_order, piece, legendre, sent)
        first += count
    data = lax.all_to_all(sent.reshape(N_DEV, 1, ROWS * 128), ("chan", "blk"), 0, 0, tiled=True)
    return map_call(m_order, sector_len, data.reshape(N_DEV * ROWS, 128))


def solution(mesh):
    placed = (
        P("chan", None, "blk", None),
        P("chan", "blk", None, None),
        P(),
        P(("chan", "blk"), None),
    )
    return jax.shard_map(
        per_device, mesh=mesh, in_specs=placed, out_specs=P(("chan", "blk"), None), check_vma=False
    )
```

```python
import functools

import jax
import jax.numpy as jnp
import ml_dtypes
import numpy as np
from jax import lax
from jax.experimental import pallas as pl
from jax.experimental.pallas import tpu as pltpu
from jax.sharding import PartitionSpec as P

M = 3072
LB = 1536
PIX = 8192
CH = 12
NSEC = 16
NSLOT = 24
NCYC = 4
N_CHAN = 4
N_BLK = 32
N_DEV = N_CHAN * N_BLK
RIDGE_FACTOR = 0.05

NA, NB, NM1, NM2 = 128, 64, 128, 24
PAIRS = 6
ROWS = 10

CHUNKS = (16, 8)
VMEM_LEG = 16 * 2**20
FETCHES = 6
ORDER = (2, 1, 3)
MOMENTS_UNROLL = 4
TOP_CODE = 32000.0
LN2 = float(np.log(2.0))

f32, bf16 = jnp.float32, jnp.bfloat16


def split_np(x):
    high = x.astype(ml_dtypes.bfloat16)
    low = (x - high.astype(np.float64)).astype(ml_dtypes.bfloat16)
    return high, low


@functools.cache
def tables():
    b, m2 = np.arange(NB)[:, None], np.arange(NM2)[None, :]
    angle = 2 * np.pi * ((b * m2) % 64) / 64
    stage1 = np.block([[np.cos(angle), -np.sin(angle)], [np.sin(angle), np.cos(angle)]])
    high, low = split_np(stage1)
    stage1 = np.concatenate([high, high, low], axis=1)
    m1 = np.arange(NM1)[None, :]
    angle = 2 * np.pi * b * m1 / PIX
    twiddle = np.concatenate([np.cos(angle), np.sin(angle)], axis=0).astype(np.float32)
    m1, a = np.arange(NM1)[:, None], np.arange(NA)[None, :]
    angle = 2 * np.pi * ((m1 * a) % 128) / 128
    stage2 = 2.0 * np.concatenate([np.cos(angle), -np.sin(angle)], axis=0)
    stage2 = np.concatenate(split_np(stage2), axis=1)
    return stage1, twiddle, stage2


def split2(x):
    high = x.astype(bf16)
    return high, (x - high.astype(f32)).astype(bf16)


def split3(x):
    high = x.astype(bf16)
    rest = x - high.astype(f32)
    mid = rest.astype(bf16)
    return high, mid, (rest - mid.astype(f32)).astype(bf16)


def dot_nn(x, y):
    return lax.dot_general(x, y, (((1,), (0,)), ((), ())), preferred_element_type=f32)


def dot_nt(x, y):
    return lax.dot_general(x, y, (((1,), (1,)), ((), ())), preferred_element_type=f32)


def fetch_kernel(source_ref, out_ref, sems):
    step = NSLOT // FETCHES
    copies = [
        pltpu.make_async_copy(source_ref.at[pl.ds(i * step, step)], out_ref.at[pl.ds(i * step, step)], sems.at[i])
        for i in range(FETCHES)
    ]
    for copy in copies:
        copy.start()
    for copy in copies:
        copy.wait()


def fetch_call(legendre):
    return pl.pallas_call(
        fetch_kernel,
        out_shape=jax.ShapeDtypeStruct(legendre.shape, legendre.dtype),
        in_specs=[pl.BlockSpec(memory_space=pl.ANY)],
        out_specs=pl.BlockSpec(memory_space=pltpu.VMEM),
        scratch_shapes=[pltpu.SemaphoreType.DMA((FETCHES,))],
        compiler_params=pltpu.CompilerParams(vmem_limit_bytes=VMEM_LEG),
        cost_estimate=pl.CostEstimate(flops=0, bytes_accessed=2 * legendre.size * 2, transcendentals=0),
    )(legendre)


def legendre_kernel(first, count, has_before, orders_ref, *refs):
    coef_refs, refs = refs[:4], refs[4:]
    leg_ref, refs = refs[0], refs[1:]
    before_ref, refs = (refs[0], refs[1:]) if has_before else (None, refs)
    out_ref, wide_ref, acc_ref = refs

    me = lax.axis_index("chan")
    own = (lax.axis_index("blk") * N_CHAN + me) * NSLOT + first

    for k in range(4):
        source = (me - k) & (N_CHAN - 1)
        for i in range(6):
            value = coef_refs[k][i].astype(f32)
            start = pl.multiple_of((source * 6 + i) * count, 8)
            for j in range(LB // 128):
                wide_ref[j, pl.ds(start, count), :] = value[:, j * 128 : (j + 1) * 128]
    if has_before:
        out_ref[...] = before_ref[...]
    else:
        out_ref[...] = jnp.zeros_like(out_ref)

    degree = (M - LB) + lax.broadcasted_iota(jnp.int32, (1, LB), 1)
    lane = lax.broadcasted_iota(jnp.int32, (64, 128), 1)
    half = lane < 64
    even_group = (lane & 32) == 0
    spare = (lane & 31) >= 24

    def octet(step, carry):
        at = first // 8 + step
        north, south = [], []
        code_row = jnp.zeros((8, 128), jnp.int32)
        for pair in range(4):
            slot = step * 8 + pair * 2
            swap = (orders_ref[own + slot] >= M // 2).astype(jnp.int32)
            top = None
            for u, slot in ((2 * pair, slot + swap), (2 * pair + 1, slot + 1 - swap)):
                m = orders_ref[own + slot]
                coef = jnp.concatenate(
                    [wide_ref[j, pl.ds(slot, 2 * CH, stride=count), :] for j in range(LB // 128)], axis=1
                )
                keep = (degree >= m).astype(f32)
                sign = (1 - 2 * ((degree + m) & 1)).astype(f32) * keep
                none = jnp.zeros((8, LB), f32)
                up = jnp.concatenate([coef * keep, none], axis=0).astype(bf16)
                down = jnp.concatenate([coef * sign, none], axis=0).astype(bf16)
                rhs = jnp.concatenate([up, up, down, down], axis=0)
                product = dot_nt(leg_ref[first + slot], rhs)
                acc_ref[u] = product
                most = jnp.max(jnp.abs(product), axis=0, keepdims=True)
                top = most if top is None else jnp.maximum(top, most)
            top = jnp.max(jnp.broadcast_to(top, (8, 128)), axis=1, keepdims=True)
            code = jnp.ceil(jnp.log(jnp.broadcast_to(jnp.maximum(top, 1e-30), (8, 128))) * (8 / LN2))
            inverse = (TOP_CODE * jnp.exp(code * (-LN2 / 8)))[0:1]
            code_row = jnp.where(lane[0:8] == 4 * at + pair, code.astype(jnp.int32), code_row)
            words = []
            for u in (2 * pair, 2 * pair + 1):
                k0, k1, k2, k3 = (acc_ref[u, pl.ds(k, 64, stride=4), :] for k in range(4))
                upper = jnp.round(jnp.where(even_group, k0, k1) * inverse).astype(jnp.int32)
                lower = jnp.round(jnp.where(even_group, k2, k3) * inverse).astype(jnp.int32)
                words.append((upper & 0xFFFF) | (lower << 16))
            north.append(jnp.where(half, words[0], pltpu.roll(words[1], 64, 1)))
            south.append(jnp.where(half, pltpu.roll(words[0], 64, 1), words[1]))
        code_row = jnp.broadcast_to(code_row[0:1], (64, 128))
        for hemi, part in enumerate((north, south)):
            base = hemi * 64 * ROWS
            for r in range(3):
                row = jnp.where(spare, pltpu.roll(part[3], 24 - 8 * r, 1), part[r])
                out_ref[pl.ds(base + 3 * at + r, 64, stride=ROWS), :] = row
            scales = out_ref[pl.ds(base + 9, 64, stride=ROWS), :]
            out_ref[pl.ds(base + 9, 64, stride=ROWS), :] = jnp.where((lane >> 2) == at, code_row, scales)
        return carry

    lax.fori_loop(0, count // 8, octet, 0, unroll=count // 8)


def legendre_call(first, count, orders, coefs, legendre, before=None):
    smem, vmem = pl.BlockSpec(memory_space=pltpu.SMEM), pl.BlockSpec(memory_space=pltpu.VMEM)
    args = [orders, *coefs, legendre] + ([] if before is None else [before])
    return pl.pallas_call(
        functools.partial(legendre_kernel, first, count, before is not None),
        out_shape=jax.ShapeDtypeStruct((N_DEV * ROWS, 128), jnp.int32),
        in_specs=[smem] + [vmem] * (len(args) - 1),
        out_specs=vmem,
        scratch_shapes=[
            pltpu.VMEM((LB // 128, 2 * CH * count, 128), f32),
            pltpu.VMEM((8, 256, 128), f32),
        ],
        compiler_params=pltpu.CompilerParams(vmem_limit_bytes=VMEM_LEG),
        cost_estimate=pl.CostEstimate(flops=count * 256 * LB * 256, bytes_accessed=count * 256 * LB * 2, transcendentals=0),
    )(*args)


def sector_kernel(lens_ref, bound_ref, hot_ref):
    hot_row = lax.broadcasted_iota(jnp.int32, (64, 128), 0)
    for k in range(NCYC):
        start = lax.broadcasted_iota(jnp.int32, (8, 128), 1) * 64
        which = jnp.zeros((8, 128), jnp.int32)
        bound = jnp.full((8, 128), PIX, jnp.int32)
        end = jnp.int32(0)
        for q in range(NSEC):
            end = end + lens_ref[k, q]
            passed = end <= start
            which = which + passed.astype(jnp.int32)
            bound = jnp.minimum(bound, jnp.where(passed, PIX, end))
        bound_ref[k * 8 : k * 8 + 8, :] = bound - start
        for h in range(2):
            hot = ((hot_row >> 4) == k) & ((hot_row & 15) == which[0:1] + h)
            hot_ref[:, (k * 2 + h) * 128 : (k * 2 + h + 1) * 128] = hot.astype(bf16)


def sector_call(lens):
    vmem = pl.BlockSpec(memory_space=pltpu.VMEM)
    return pl.pallas_call(
        sector_kernel,
        out_shape=[
            jax.ShapeDtypeStruct((NCYC * 8, 128), jnp.int32),
            jax.ShapeDtypeStruct((64, 2 * NCYC * 128), bf16),
        ],
        in_specs=[pl.BlockSpec(memory_space=pltpu.SMEM)],
        out_specs=[vmem, vmem],
        compiler_params=pltpu.CompilerParams(vmem_limit_bytes=VMEM_LEG),
    )(lens)


def map_kernel(
    orders_ref, data_ref, lane_len_ref, stage1_ref, twiddle_ref, stage2_ref, bound_ref, hot_ref, out_ref,
    pair_ref, place_ref, turned_ref, map_ref, part_ref, sums_ref, cov_ref, spread_ref, comb_ref, final_ref,
):
    lane = lax.broadcasted_iota(jnp.int32, (N_DEV, 128), 1)
    which = (lane & 31) >> 3
    scales = data_ref[pl.ds(9, N_DEV, stride=ROWS), :]
    for octet in range(3):
        words = [data_ref[pl.ds(3 * octet + r, N_DEV, stride=ROWS), :] for r in range(3)]
        rolled = [pltpu.roll(words[r], 128 - (24 - 8 * r), 1) for r in range(3)]
        words.append(jnp.where(which == 0, rolled[0], jnp.where(which == 1, rolled[1], rolled[2])))
        for r in range(4):
            pair = 4 * octet + r
            scale = jnp.broadcast_to(scales[:, pair : pair + 1], (N_DEV, 128))
            pair_ref[pair * N_DEV : (pair + 1) * N_DEV, :] = jnp.where(which == 3, scale, words[r])

    def place(src, carry):
        base = ((src & (N_BLK - 1)) * N_CHAN + (src >> 5)) * NSLOT
        for pair in range(NSLOT // 2):
            m = orders_ref[base + 2 * pair]
            row = pair_ref[pl.ds(pair * N_DEV + src, 1), :]
            place_ref[pl.ds(m, 1), :] = row
            place_ref[pl.ds(M - 1 - m, 1), :] = row
        return carry

    lax.fori_loop(0, N_DEV, place, 0, unroll=2)

    for m2 in range(NM2):
        block = place_ref[m2 * 128 : (m2 + 1) * 128, :].T
        side = 64 * (m2 // (NM2 // 2))
        scale = jnp.exp(block[side + 24 : side + 25].astype(f32) * (LN2 / 8)) * (1.0 / TOP_CODE)
        if m2 == 0:
            scale = jnp.where(lax.broadcasted_iota(jnp.int32, (1, 128), 1) == 0, 0.5 * scale, scale)
        for k in range(2):
            word = block[side + k * 32 : side + k * 32 + 24]
            for h, code in enumerate(((word << 16) >> 16, word >> 16)):
                start = (k + 2 * h) * 2 * CH * NM2 + m2
                turned_ref[pl.ds(start, 2 * CH, stride=NM2), :] = code.astype(f32) * scale

    stage1 = stage1_ref[...]

    def transform(i, carry):
        tc, ts = twiddle_ref[0:64, :], twiddle_ref[64:128, :]
        outer = []
        for pair in range(PAIRS):
            parts = []
            for j in range(2):
                start = pl.multiple_of((i * PAIRS + pair) * 96 + j * 48, 16)
                high, low = split2(turned_ref[pl.ds(start, 48), :])
                parts.append(jnp.concatenate([high, low, high], axis=0))
            inner = dot_nn(stage1, jnp.concatenate(parts, axis=1))
            for j in range(2):
                re, im = inner[0:64, j * 128 : (j + 1) * 128], inner[64:128, j * 128 : (j + 1) * 128]
                outer.append(jnp.concatenate([re * tc - im * ts, re * ts + im * tc], axis=1))
        high, low = split2(jnp.concatenate(outer, axis=0))
        both = dot_nn(high, stage2_ref[...])
        maps = both[:, 0:128] + (both[:, 128:256] + dot_nn(low, stage2_ref[:, 0:128]))
        map_ref[pl.ds(pl.multiple_of(i * PAIRS * 128, 128), PAIRS * 128), :] = maps
        return carry

    lax.fori_loop(0, NCYC * CH // (2 * PAIRS), transform, 0, unroll=4)

    chunk = lax.broadcasted_iota(jnp.int32, (64, 128), 1)
    offset = lax.broadcasted_iota(jnp.int32, (64, 128), 0)
    def moments(k, carry):
        inside = offset < bound_ref[pl.ds(pl.multiple_of(k * 8, 8), 1), :]
        base = pl.multiple_of(k * CH * 64, 64)
        for i in range(CH):
            value = map_ref[pl.ds(base + i * 64, 64), :]
            low = jnp.where(inside, value, 0.0)
            high = jnp.where(inside, 0.0, value)
            for j in range(i, CH):
                other = map_ref[pl.ds(base + j * 64, 64), :]
                for h, part in enumerate((low, high)):
                    product = part * other
                    pairs = [product[b * 16 : b * 16 + 8] + product[b * 16 + 8 : b * 16 + 16] for b in range(4)]
                    at = (h * CH + i) * 128 + j * 8
                    part_ref[at : at + 8, :] = (pairs[0] + pairs[1]) + (pairs[2] + pairs[3])
        for h in range(2):
            for i in range(CH):
                at = (h * CH + i) * 128
                summed = [part_ref[pl.ds(at + b, 16, stride=8), :] for b in range(8)]
                while len(summed) > 1:
                    summed = [summed[b] + summed[b + 1] for b in range(0, len(summed), 2)]
                sums_ref[pl.ds(pl.multiple_of((k * 2 + h) * CH * 16, 16) + i * 16, 16), :] = summed[0]
        return carry

    lax.fori_loop(0, NCYC, moments, 0, unroll=MOMENTS_UNROLL)
    sums = jnp.concatenate([sums_ref[g * CH * 16 : (g + 1) * CH * 16, :] for g in range(2 * NCYC)], axis=1)
    total = None
    for part in split3(sums):
        product = dot_nt(part, hot_ref[...])
        total = product if total is None else total + product
    cov_ref[...] = total
    for i in range(CH):
        for j in range(i + 1, CH):
            cov_ref[j * 16 + i : j * 16 + i + 1, :] = cov_ref[i * 16 + j : i * 16 + j + 1, :]

    scale = 1.0 / lane_len_ref[...].astype(f32)
    sub = lax.broadcasted_iota(jnp.int32, (16, 64), 0)
    mat = [cov_ref[i * 16 : (i + 1) * 16, :] * scale for i in range(CH)]
    trace = mat[0][0:1]
    for i in range(1, CH):
        trace = trace + mat[i][i : i + 1]
    ridge = trace * (RIDGE_FACTOR / CH)
    for i in range(CH):
        mat[i] = jnp.where(sub == CH, 1.0, jnp.where(sub == i, mat[i] + ridge, mat[i]))
    for p in range(CH):
        pivot = mat[p] / mat[p][p : p + 1]
        for i in range(CH):
            mat[i] = pivot if i == p else mat[i] - mat[i][p : p + 1] * pivot
    solved = [mat[i][CH : CH + 1] for i in range(CH)]
    norm = solved[0]
    for i in range(1, CH):
        norm = norm + solved[i]
    weights = jnp.concatenate([s / norm for s in solved] + [jnp.zeros((4, 64), f32)], axis=0)
    spread = dot_nn(jnp.concatenate(split3(weights), axis=0), hot_ref[...])
    spread = spread[0:16] + (spread[16:32] + spread[32:48])
    for g in range(2 * NCYC):
        spread_ref[g * 16 : (g + 1) * 16, :] = spread[:, g * 128 : (g + 1) * 128]

    def combine(k, carry):
        inside = offset < bound_ref[pl.ds(pl.multiple_of(k * 8, 8), 1), :]
        chunk_weights = [spread_ref[pl.ds(pl.multiple_of((k * 2 + h) * 16, 16), 16), :] for h in range(2)]
        base = pl.multiple_of(k * CH * 64, 64)
        total = jnp.zeros((64, 128), f32)
        for c in range(CH):
            weight = jnp.where(inside, chunk_weights[0][c : c + 1], chunk_weights[1][c : c + 1])
            total = total + weight * map_ref[pl.ds(base + c * 64, 64), :]
        wide = jnp.concatenate([total, total], axis=0).T
        comb_ref[k] = wide
        pair = jnp.where(chunk < 64, comb_ref[k, pl.ds(0, 64, stride=2), :], comb_ref[k, pl.ds(1, 64, stride=2), :])
        final_ref[pl.ds(k, 64, stride=NCYC), :] = pair
        return carry

    lax.fori_loop(0, NCYC, combine, 0, unroll=4)
    for i in range(64):
        out_ref[:, i * 128 : (i + 1) * 128] = final_ref[i * NCYC : (i + 1) * NCYC, :]


def map_call(orders, lens, data, sectors):
    stage1, twiddle, stage2 = tables()
    smem, vmem = pl.BlockSpec(memory_space=pltpu.SMEM), pl.BlockSpec(memory_space=pltpu.VMEM)
    return pl.pallas_call(
        map_kernel,
        out_shape=jax.ShapeDtypeStruct((NCYC, PIX), f32),
        in_specs=[smem] + [vmem] * 7,
        out_specs=vmem,
        scratch_shapes=[
            pltpu.VMEM((NSLOT // 2 * N_DEV, 128), jnp.int32),
            pltpu.VMEM((M, 128), jnp.int32),
            pltpu.VMEM((NCYC * 2 * CH * NM2, 128), f32),
            pltpu.VMEM((NCYC * CH * 64, 128), f32),
            pltpu.VMEM((2 * CH * 128, 128), f32),
            pltpu.VMEM((2 * NCYC * CH * 16, 128), f32),
            pltpu.VMEM((CH * 16, 64), f32),
            pltpu.VMEM((2 * NCYC * 16, 128), f32),
            pltpu.VMEM((NCYC, 128, 128), f32),
            pltpu.VMEM((64 * NCYC, 128), f32),
        ],
        compiler_params=pltpu.CompilerParams(vmem_limit_bytes=40 * 2**20),
    )(orders, data, lens.reshape(1, NCYC * NSEC), stage1, twiddle, stage2, *sectors)


def slices_kernel(coef_ref, *refs):
    outs, sems = refs[:-1], refs[-1]
    me = lax.axis_index("chan")
    copies, first = [], 0
    for n, count in enumerate(CHUNKS):
        for k in (2, 1, 3, 0):
            source = coef_ref.at[:, (me + k) & (N_CHAN - 1), pl.ds(first, count)]
            copies.append(pltpu.make_async_copy(source, outs[n * N_CHAN + k], sems.at[n * N_CHAN + k]))
        first += count
    for copy in copies:
        copy.start()
    for copy in copies:
        copy.wait()


def cut(coeffs):
    shapes = [jax.ShapeDtypeStruct((6, count, LB), bf16) for count in CHUNKS for _ in range(N_CHAN)]
    pieces = pl.pallas_call(
        slices_kernel,
        out_shape=shapes,
        in_specs=[pl.BlockSpec(memory_space=pl.ANY)],
        out_specs=[pl.BlockSpec(memory_space=pltpu.VMEM)] * len(shapes),
        scratch_shapes=[pltpu.SemaphoreType.DMA((len(shapes),))],
        compiler_params=pltpu.CompilerParams(vmem_limit_bytes=VMEM_LEG),
    )(coeffs.reshape(6, N_CHAN, NSLOT, LB))
    return [list(pieces[n * N_CHAN : (n + 1) * N_CHAN]) for n in range(len(CHUNKS))]


def send(pieces):
    pieces = list(pieces)
    for k in ORDER:
        pieces[k] = lax.ppermute(pieces[k], "chan", [(i, (i + k) % N_CHAN) for i in range(N_CHAN)])
    return pieces


def per_device(coeffs, legendre, m_order, sector_len):
    early, late = cut(coeffs)
    early = send(early)
    legendre, late = lax.optimization_barrier((fetch_call(legendre[0]), late))
    pieces = [early, send(late)]
    sent, first = None, 0
    for count, piece in zip(CHUNKS, pieces):
        sent = legendre_call(first, count, m_order, piece, legendre, sent)
        first += count
    data = lax.all_to_all(sent.reshape(N_DEV, 1, ROWS * 128), ("chan", "blk"), 0, 0, tiled=True)
    return map_call(m_order, sector_len, data.reshape(N_DEV * ROWS, 128), sector_call(sector_len))


def solution(mesh):
    placed = (
        P("chan", None, "blk", None),
        P("chan", "blk", None, None),
        P(),
        P(("chan", "blk"), None),
    )
    return jax.shard_map(
        per_device, mesh=mesh, in_specs=placed, out_specs=P(("chan", "blk"), None), check_vma=False
    )
```

```python
import functools

import jax
import jax.numpy as jnp
import ml_dtypes
import numpy as np
from jax import lax
from jax.experimental import pallas as pl
from jax.experimental.pallas import tpu as pltpu
from jax.sharding import PartitionSpec as P

M = 3072
LB = 1536
PIX = 8192
CH = 12
NSEC = 16
NSLOT = 24
NCYC = 4
N_CHAN = 4
N_BLK = 32
N_DEV = N_CHAN * N_BLK
RIDGE_FACTOR = 0.05

NA, NB, NM1, NM2 = 128, 64, 128, 24
PAIRS = 6
ROWS = 10

CHUNKS = (16, 8)
VMEM_LEG = 16 * 2**20
FETCHES = 6
ORDER = (1, 3, 2)
MOMENTS_UNROLL = 4
TOP_CODE = 32000.0
LN2 = float(np.log(2.0))

f32, bf16 = jnp.float32, jnp.bfloat16


def split_np(x):
    high = x.astype(ml_dtypes.bfloat16)
    low = (x - high.astype(np.float64)).astype(ml_dtypes.bfloat16)
    return high, low


@functools.cache
def tables():
    b, m2 = np.arange(NB)[:, None], np.arange(NM2)[None, :]
    angle = 2 * np.pi * ((b * m2) % 64) / 64
    stage1 = np.block([[np.cos(angle), -np.sin(angle)], [np.sin(angle), np.cos(angle)]])
    high, low = split_np(stage1)
    stage1 = np.concatenate([high, high, low], axis=1)
    m1 = np.arange(NM1)[None, :]
    angle = 2 * np.pi * b * m1 / PIX
    twiddle = np.concatenate([np.cos(angle), np.sin(angle)], axis=0).astype(np.float32)
    m1, a = np.arange(NM1)[:, None], np.arange(NA)[None, :]
    angle = 2 * np.pi * ((m1 * a) % 128) / 128
    stage2 = 2.0 * np.concatenate([np.cos(angle), -np.sin(angle)], axis=0)
    stage2 = np.concatenate(split_np(stage2), axis=1)
    return stage1, twiddle, stage2


def split2(x):
    high = x.astype(bf16)
    return high, (x - high.astype(f32)).astype(bf16)


def split3(x):
    high = x.astype(bf16)
    rest = x - high.astype(f32)
    mid = rest.astype(bf16)
    return high, mid, (rest - mid.astype(f32)).astype(bf16)


def dot_nn(x, y):
    return lax.dot_general(x, y, (((1,), (0,)), ((), ())), preferred_element_type=f32)


def dot_nt(x, y):
    return lax.dot_general(x, y, (((1,), (1,)), ((), ())), preferred_element_type=f32)


def fetch_kernel(source_ref, out_ref, sems):
    step = NSLOT // FETCHES
    copies = [
        pltpu.make_async_copy(source_ref.at[pl.ds(i * step, step)], out_ref.at[pl.ds(i * step, step)], sems.at[i])
        for i in range(FETCHES)
    ]
    for copy in copies:
        copy.start()
    for copy in copies:
        copy.wait()


def fetch_call(legendre):
    return pl.pallas_call(
        fetch_kernel,
        out_shape=jax.ShapeDtypeStruct(legendre.shape, legendre.dtype),
        in_specs=[pl.BlockSpec(memory_space=pl.ANY)],
        out_specs=pl.BlockSpec(memory_space=pltpu.VMEM),
        scratch_shapes=[pltpu.SemaphoreType.DMA((FETCHES,))],
        compiler_params=pltpu.CompilerParams(vmem_limit_bytes=VMEM_LEG),
        cost_estimate=pl.CostEstimate(flops=0, bytes_accessed=2 * legendre.size * 2, transcendentals=0),
    )(legendre)


def legendre_kernel(first, count, has_before, orders_ref, *refs):
    coef_refs, refs = refs[:4], refs[4:]
    leg_ref, refs = refs[0], refs[1:]
    before_ref, refs = (refs[0], refs[1:]) if has_before else (None, refs)
    out_ref, wide_ref, acc_ref = refs

    me = lax.axis_index("chan")
    own = (lax.axis_index("blk") * N_CHAN + me) * NSLOT + first

    for k in range(4):
        source = (me - k) & (N_CHAN - 1)
        for i in range(6):
            value = coef_refs[k][i].astype(f32)
            start = pl.multiple_of((source * 6 + i) * count, 8)
            for j in range(LB // 128):
                wide_ref[j, pl.ds(start, count), :] = value[:, j * 128 : (j + 1) * 128]
    if has_before:
        out_ref[...] = before_ref[...]
    else:
        out_ref[...] = jnp.zeros_like(out_ref)

    degree = (M - LB) + lax.broadcasted_iota(jnp.int32, (1, LB), 1)
    lane = lax.broadcasted_iota(jnp.int32, (64, 128), 1)
    half = lane < 64
    even_group = (lane & 32) == 0
    spare = (lane & 31) >= 24

    def octet(step, carry):
        at = first // 8 + step
        north, south = [], []
        code_row = jnp.zeros((8, 128), jnp.int32)
        for pair in range(4):
            slot = step * 8 + pair * 2
            swap = (orders_ref[own + slot] >= M // 2).astype(jnp.int32)
            top = None
            for u, slot in ((2 * pair, slot + swap), (2 * pair + 1, slot + 1 - swap)):
                m = orders_ref[own + slot]
                coef = jnp.concatenate(
                    [wide_ref[j, pl.ds(slot, 2 * CH, stride=count), :] for j in range(LB // 128)], axis=1
                )
                keep = (degree >= m).astype(f32)
                sign = (1 - 2 * ((degree + m) & 1)).astype(f32) * keep
                none = jnp.zeros((8, LB), f32)
                up = jnp.concatenate([coef * keep, none], axis=0).astype(bf16)
                down = jnp.concatenate([coef * sign, none], axis=0).astype(bf16)
                rhs = jnp.concatenate([up, up, down, down], axis=0)
                product = dot_nt(leg_ref[first + slot], rhs)
                acc_ref[u] = product
                most = jnp.max(jnp.abs(product), axis=0, keepdims=True)
                top = most if top is None else jnp.maximum(top, most)
            top = jnp.max(jnp.broadcast_to(top, (8, 128)), axis=1, keepdims=True)
            code = jnp.ceil(jnp.log(jnp.broadcast_to(jnp.maximum(top, 1e-30), (8, 128))) * (8 / LN2))
            inverse = (TOP_CODE * jnp.exp(code * (-LN2 / 8)))[0:1]
            code_row = jnp.where(lane[0:8] == 4 * at + pair, code.astype(jnp.int32), code_row)
            words = []
            for u in (2 * pair, 2 * pair + 1):
                k0, k1, k2, k3 = (acc_ref[u, pl.ds(k, 64, stride=4), :] for k in range(4))
                upper = jnp.round(jnp.where(even_group, k0, k1) * inverse).astype(jnp.int32)
                lower = jnp.round(jnp.where(even_group, k2, k3) * inverse).astype(jnp.int32)
                words.append((upper & 0xFFFF) | (lower << 16))
            north.append(jnp.where(half, words[0], pltpu.roll(words[1], 64, 1)))
            south.append(jnp.where(half, pltpu.roll(words[0], 64, 1), words[1]))
        code_row = jnp.broadcast_to(code_row[0:1], (64, 128))
        for hemi, part in enumerate((north, south)):
            base = hemi * 64 * ROWS
            for r in range(3):
                row = jnp.where(spare, pltpu.roll(part[3], 24 - 8 * r, 1), part[r])
                out_ref[pl.ds(base + 3 * at + r, 64, stride=ROWS), :] = row
            scales = out_ref[pl.ds(base + 9, 64, stride=ROWS), :]
            out_ref[pl.ds(base + 9, 64, stride=ROWS), :] = jnp.where((lane >> 2) == at, code_row, scales)
        return carry

    lax.fori_loop(0, count // 8, octet, 0, unroll=count // 8)


def legendre_call(first, count, orders, coefs, legendre, before=None):
    smem, vmem = pl.BlockSpec(memory_space=pltpu.SMEM), pl.BlockSpec(memory_space=pltpu.VMEM)
    args = [orders, *coefs, legendre] + ([] if before is None else [before])
    return pl.pallas_call(
        functools.partial(legendre_kernel, first, count, before is not None),
        out_shape=jax.ShapeDtypeStruct((N_DEV * ROWS, 128), jnp.int32),
        in_specs=[smem] + [vmem] * (len(args) - 1),
        out_specs=vmem,
        scratch_shapes=[
            pltpu.VMEM((LB // 128, 2 * CH * count, 128), f32),
            pltpu.VMEM((8, 256, 128), f32),
        ],
        compiler_params=pltpu.CompilerParams(vmem_limit_bytes=VMEM_LEG),
        cost_estimate=pl.CostEstimate(flops=count * 256 * LB * 256, bytes_accessed=count * 256 * LB * 2, transcendentals=0),
    )(*args)


def sector_kernel(lens_ref, bound_ref, hot_ref):
    hot_row = lax.broadcasted_iota(jnp.int32, (64, 128), 0)
    for k in range(NCYC):
        start = lax.broadcasted_iota(jnp.int32, (8, 128), 1) * 64
        which = jnp.zeros((8, 128), jnp.int32)
        bound = jnp.full((8, 128), PIX, jnp.int32)
        end = jnp.int32(0)
        for q in range(NSEC):
            end = end + lens_ref[k, q]
            passed = end <= start
            which = which + passed.astype(jnp.int32)
            bound = jnp.minimum(bound, jnp.where(passed, PIX, end))
        bound_ref[k * 8 : k * 8 + 8, :] = bound - start
        for h in range(2):
            hot = ((hot_row >> 4) == k) & ((hot_row & 15) == which[0:1] + h)
            hot_ref[:, (k * 2 + h) * 128 : (k * 2 + h + 1) * 128] = hot.astype(bf16)


def sector_call(lens):
    vmem = pl.BlockSpec(memory_space=pltpu.VMEM)
    return pl.pallas_call(
        sector_kernel,
        out_shape=[
            jax.ShapeDtypeStruct((NCYC * 8, 128), jnp.int32),
            jax.ShapeDtypeStruct((64, 2 * NCYC * 128), bf16),
        ],
        in_specs=[pl.BlockSpec(memory_space=pltpu.SMEM)],
        out_specs=[vmem, vmem],
        compiler_params=pltpu.CompilerParams(vmem_limit_bytes=VMEM_LEG),
    )(lens)


def map_kernel(
    orders_ref, data_ref, lane_len_ref, stage1_ref, twiddle_ref, stage2_ref, bound_ref, hot_ref, out_ref,
    pair_ref, place_ref, turned_ref, map_ref, part_ref, sums_ref, cov_ref, spread_ref, comb_ref, final_ref,
):
    lane = lax.broadcasted_iota(jnp.int32, (N_DEV, 128), 1)
    which = (lane & 31) >> 3
    scales = data_ref[pl.ds(9, N_DEV, stride=ROWS), :]
    for octet in range(3):
        words = [data_ref[pl.ds(3 * octet + r, N_DEV, stride=ROWS), :] for r in range(3)]
        rolled = [pltpu.roll(words[r], 128 - (24 - 8 * r), 1) for r in range(3)]
        words.append(jnp.where(which == 0, rolled[0], jnp.where(which == 1, rolled[1], rolled[2])))
        for r in range(4):
            pair = 4 * octet + r
            scale = jnp.broadcast_to(scales[:, pair : pair + 1], (N_DEV, 128))
            pair_ref[pair * N_DEV : (pair + 1) * N_DEV, :] = jnp.where(which == 3, scale, words[r])

    def place(src, carry):
        base = ((src & (N_BLK - 1)) * N_CHAN + (src >> 5)) * NSLOT
        for pair in range(NSLOT // 2):
            m = orders_ref[base + 2 * pair]
            row = pair_ref[pl.ds(pair * N_DEV + src, 1), :]
            place_ref[pl.ds(m, 1), :] = row
            place_ref[pl.ds(M - 1 - m, 1), :] = row
        return carry

    lax.fori_loop(0, N_DEV, place, 0, unroll=8)

    for m2 in range(NM2):
        block = place_ref[m2 * 128 : (m2 + 1) * 128, :].T
        side = 64 * (m2 // (NM2 // 2))
        scale = jnp.exp(block[side + 24 : side + 25].astype(f32) * (LN2 / 8)) * (1.0 / TOP_CODE)
        if m2 == 0:
            scale = jnp.where(lax.broadcasted_iota(jnp.int32, (1, 128), 1) == 0, 0.5 * scale, scale)
        for k in range(2):
            word = block[side + k * 32 : side + k * 32 + 24]
            for h, code in enumerate(((word << 16) >> 16, word >> 16)):
                start = (k + 2 * h) * 2 * CH * NM2 + m2
                turned_ref[pl.ds(start, 2 * CH, stride=NM2), :] = code.astype(f32) * scale

    stage1 = stage1_ref[...]

    def transform(i, carry):
        tc, ts = twiddle_ref[0:64, :], twiddle_ref[64:128, :]
        outer = []
        for pair in range(PAIRS):
            parts = []
            for j in range(2):
                start = pl.multiple_of((i * PAIRS + pair) * 96 + j * 48, 16)
                high, low = split2(turned_ref[pl.ds(start, 48), :])
                parts.append(jnp.concatenate([high, low, high], axis=0))
            inner = dot_nn(stage1, jnp.concatenate(parts, axis=1))
            for j in range(2):
                re, im = inner[0:64, j * 128 : (j + 1) * 128], inner[64:128, j * 128 : (j + 1) * 128]
                outer.append(jnp.concatenate([re * tc - im * ts, re * ts + im * tc], axis=1))
        high, low = split2(jnp.concatenate(outer, axis=0))
        both = dot_nn(high, stage2_ref[...])
        maps = both[:, 0:128] + (both[:, 128:256] + dot_nn(low, stage2_ref[:, 0:128]))
        map_ref[pl.ds(pl.multiple_of(i * PAIRS * 128, 128), PAIRS * 128), :] = maps
        return carry

    lax.fori_loop(0, NCYC * CH // (2 * PAIRS), transform, 0, unroll=4)

    chunk = lax.broadcasted_iota(jnp.int32, (64, 128), 1)
    offset = lax.broadcasted_iota(jnp.int32, (64, 128), 0)
    def moments(k, carry):
        inside = offset < bound_ref[pl.ds(pl.multiple_of(k * 8, 8), 1), :]
        base = pl.multiple_of(k * CH * 64, 64)
        for i in range(CH):
            value = map_ref[pl.ds(base + i * 64, 64), :]
            low = jnp.where(inside, value, 0.0)
            high = jnp.where(inside, 0.0, value)
            for j in range(i, CH):
                other = map_ref[pl.ds(base + j * 64, 64), :]
                for h, part in enumerate((low, high)):
                    product = part * other
                    pairs = [product[b * 16 : b * 16 + 8] + product[b * 16 + 8 : b * 16 + 16] for b in range(4)]
                    at = (h * CH + i) * 128 + j * 8
                    part_ref[at : at + 8, :] = (pairs[0] + pairs[1]) + (pairs[2] + pairs[3])
        for h in range(2):
            for i in range(CH):
                at = (h * CH + i) * 128
                summed = [part_ref[pl.ds(at + b, 16, stride=8), :] for b in range(8)]
                while len(summed) > 1:
                    summed = [summed[b] + summed[b + 1] for b in range(0, len(summed), 2)]
                sums_ref[pl.ds(pl.multiple_of((k * 2 + h) * CH * 16, 16) + i * 16, 16), :] = summed[0]
        return carry

    lax.fori_loop(0, NCYC, moments, 0, unroll=MOMENTS_UNROLL)
    sums = jnp.concatenate([sums_ref[g * CH * 16 : (g + 1) * CH * 16, :] for g in range(2 * NCYC)], axis=1)
    total = None
    for part in split3(sums):
        product = dot_nt(part, hot_ref[...])
        total = product if total is None else total + product
    cov_ref[...] = total
    for i in range(CH):
        for j in range(i + 1, CH):
            cov_ref[j * 16 + i : j * 16 + i + 1, :] = cov_ref[i * 16 + j : i * 16 + j + 1, :]

    scale = 1.0 / lane_len_ref[...].astype(f32)
    sub = lax.broadcasted_iota(jnp.int32, (16, 64), 0)
    mat = [cov_ref[i * 16 : (i + 1) * 16, :] * scale for i in range(CH)]
    trace = mat[0][0:1]
    for i in range(1, CH):
        trace = trace + mat[i][i : i + 1]
    ridge = trace * (RIDGE_FACTOR / CH)
    for i in range(CH):
        mat[i] = jnp.where(sub == CH, 1.0, jnp.where(sub == i, mat[i] + ridge, mat[i]))
    for p in range(CH):
        pivot = mat[p] / mat[p][p : p + 1]
        for i in range(CH):
            mat[i] = pivot if i == p else mat[i] - mat[i][p : p + 1] * pivot
    solved = [mat[i][CH : CH + 1] for i in range(CH)]
    norm = solved[0]
    for i in range(1, CH):
        norm = norm + solved[i]
    weights = jnp.concatenate([s / norm for s in solved] + [jnp.zeros((4, 64), f32)], axis=0)
    spread = dot_nn(jnp.concatenate(split3(weights), axis=0), hot_ref[...])
    spread = spread[0:16] + (spread[16:32] + spread[32:48])
    for g in range(2 * NCYC):
        spread_ref[g * 16 : (g + 1) * 16, :] = spread[:, g * 128 : (g + 1) * 128]

    def combine(k, carry):
        inside = offset < bound_ref[pl.ds(pl.multiple_of(k * 8, 8), 1), :]
        chunk_weights = [spread_ref[pl.ds(pl.multiple_of((k * 2 + h) * 16, 16), 16), :] for h in range(2)]
        base = pl.multiple_of(k * CH * 64, 64)
        total = jnp.zeros((64, 128), f32)
        for c in range(CH):
            weight = jnp.where(inside, chunk_weights[0][c : c + 1], chunk_weights[1][c : c + 1])
            total = total + weight * map_ref[pl.ds(base + c * 64, 64), :]
        wide = jnp.concatenate([total, total], axis=0).T
        comb_ref[k] = wide
        pair = jnp.where(chunk < 64, comb_ref[k, pl.ds(0, 64, stride=2), :], comb_ref[k, pl.ds(1, 64, stride=2), :])
        final_ref[pl.ds(k, 64, stride=NCYC), :] = pair
        return carry

    lax.fori_loop(0, NCYC, combine, 0, unroll=4)
    for i in range(64):
        out_ref[:, i * 128 : (i + 1) * 128] = final_ref[i * NCYC : (i + 1) * NCYC, :]


def map_call(orders, lens, data, sectors):
    stage1, twiddle, stage2 = tables()
    smem, vmem = pl.BlockSpec(memory_space=pltpu.SMEM), pl.BlockSpec(memory_space=pltpu.VMEM)
    return pl.pallas_call(
        map_kernel,
        out_shape=jax.ShapeDtypeStruct((NCYC, PIX), f32),
        in_specs=[smem] + [vmem] * 7,
        out_specs=vmem,
        scratch_shapes=[
            pltpu.VMEM((NSLOT // 2 * N_DEV, 128), jnp.int32),
            pltpu.VMEM((M, 128), jnp.int32),
            pltpu.VMEM((NCYC * 2 * CH * NM2, 128), f32),
            pltpu.VMEM((NCYC * CH * 64, 128), f32),
            pltpu.VMEM((2 * CH * 128, 128), f32),
            pltpu.VMEM((2 * NCYC * CH * 16, 128), f32),
            pltpu.VMEM((CH * 16, 64), f32),
            pltpu.VMEM((2 * NCYC * 16, 128), f32),
            pltpu.VMEM((NCYC, 128, 128), f32),
            pltpu.VMEM((64 * NCYC, 128), f32),
        ],
        compiler_params=pltpu.CompilerParams(vmem_limit_bytes=40 * 2**20),
    )(orders, data, lens.reshape(1, NCYC * NSEC), stage1, twiddle, stage2, *sectors)


def slices_kernel(coef_ref, *refs):
    outs, sems = refs[:-1], refs[-1]
    me = lax.axis_index("chan")
    copies, first = [], 0
    for n, count in enumerate(CHUNKS):
        for k in (2, 1, 3, 0):
            source = coef_ref.at[:, (me + k) & (N_CHAN - 1), pl.ds(first, count)]
            copies.append(pltpu.make_async_copy(source, outs[n * N_CHAN + k], sems.at[n * N_CHAN + k]))
        first += count
    for copy in copies:
        copy.start()
    for copy in copies:
        copy.wait()


def cut(coeffs):
    shapes = [jax.ShapeDtypeStruct((6, count, LB), bf16) for count in CHUNKS for _ in range(N_CHAN)]
    pieces = pl.pallas_call(
        slices_kernel,
        out_shape=shapes,
        in_specs=[pl.BlockSpec(memory_space=pl.ANY)],
        out_specs=[pl.BlockSpec(memory_space=pltpu.VMEM)] * len(shapes),
        scratch_shapes=[pltpu.SemaphoreType.DMA((len(shapes),))],
        compiler_params=pltpu.CompilerParams(vmem_limit_bytes=VMEM_LEG),
    )(coeffs.reshape(6, N_CHAN, NSLOT, LB))
    return [list(pieces[n * N_CHAN : (n + 1) * N_CHAN]) for n in range(len(CHUNKS))]


def send(pieces):
    pieces = list(pieces)
    for k in ORDER:
        pieces[k] = lax.ppermute(pieces[k], "chan", [(i, (i + k) % N_CHAN) for i in range(N_CHAN)])
    return pieces


def per_device(coeffs, legendre, m_order, sector_len):
    early, late = cut(coeffs)
    early = send(early)
    legendre, late = lax.optimization_barrier((fetch_call(legendre[0]), late))
    pieces = [early, send(late)]
    sent, first = None, 0
    for count, piece in zip(CHUNKS, pieces):
        sent = legendre_call(first, count, m_order, piece, legendre, sent)
        first += count
    data = lax.all_to_all(sent.reshape(N_DEV, 1, ROWS * 128), ("chan", "blk"), 0, 0, tiled=True)
    return map_call(m_order, sector_len, data.reshape(N_DEV * ROWS, 128), sector_call(sector_len))


def solution(mesh):
    placed = (
        P("chan", None, "blk", None),
        P("chan", "blk", None, None),
        P(),
        P(("chan", "blk"), None),
    )
    return jax.shard_map(
        per_device, mesh=mesh, in_specs=placed, out_specs=P(("chan", "blk"), None), check_vma=False
    )
```
